32 devices in a mesh: section: 8 (over z, y), expert: 2 (over core), shard: 2 (over x).
Axes of the slice: x: 2, y: 2, z: 4, core: 2. Of those that a mesh axis runs over, the one named last changes fastest.
Arguments:
- routes: int32 [8, 4, 64, 2], P('section', None, 'expert'), may hold values from 0 to 7, as said below
- route_probs: float32 [8, 4, 64, 2], P('section', None, 'expert'), may hold values from 0.2 to 1
- example_ids: int32 [4, 2, 32], P(None, 'expert'), may hold values from 0 to 1, never falling along the last dimension, each value on 1 to 24 neighbouring positions
- top_cotangent: bfloat16 [4, 64, 6144], P(None, 'expert', 'shard'), may hold values from -6 to 6
- branch_cotangent: bfloat16 [8, 4, 64, 6144], P('section', None, 'expert', 'shard'), may hold values from -4 to 4
- hidden_acts: bfloat16 [8, 2, 4, 32, 16384], P('section', 'expert', None, None, 'shard'), may hold values from -6 to 6
- basis_hidden: bfloat16 [8, 2, 16384, 256], P('section', 'expert', 'shard'), may hold values from -0.046875 to 0.046875
- basis_model: bfloat16 [8, 2, 6144, 1024], P('section', 'expert', 'shard'), may hold values from -0.078125 to 0.078125
Outputs:
- eigen_correction: float32 [8, 2, 256, 1024], P('section', 'expert', None, 'shard')
The draws below stay inside these ranges and needn't reach their ends.
Inputs may be any that keep to these rules, and one draw needn't show every extreme that they name: `routes`: each token names 2 different experts of the 8. Within the 32 tokens of one owner in one micro-batch no expert is named more than 16 times, and exactly one expert is named 16 times. In one micro-batch of every layer that expert is the same for every owner and is below 2. `example_ids`: Non-decreasing along each owner's 32 tokens of a micro-batch; each example has 1 to 24 tokens.
All inputs are finite; a program needn't handle non-finite values.
Results may differ from the reference program's by a relative error of at most 0.0047.
Values may be sent and summed in bfloat16 or wider, within the bound.
A program may use at most 128 MiB of HBM per device.

```python
import math
import jax
import jax.numpy as jnp
import numpy as np
from jax import lax

D = 6144
FF = 16384
ROUTED = 8
TOP = 2
MB = 4
TOK_MB = 32
SEQS = 2
KI = 256
KJ = 1024
SECTIONS = 8
EXPERTS = 2
OWNERS = 2
TOKENS = 64
CAP = 16
SLOTS = 32
LONGEST = 24
N_EXPERT = 2


def route_block(block_key, hot_expert):
    key_list = jax.random.split(block_key, 4)
    token_rank = jnp.arange(TOK_MB, dtype=jnp.int32)
    order_score = jax.random.randint(key_list[0], (TOK_MB,), 0, 1 << 20) * TOK_MB + token_rank
    token_order = jnp.argsort(order_score).astype(jnp.int32)
    others = ROUTED - 1
    name_count = TOK_MB + CAP
    spread = name_count // (3 * others)
    cut_points = jnp.arange(1, others, dtype=jnp.int32) * name_count // others
    cut_points = cut_points + jax.random.randint(key_list[1], (others - 1,), -spread, spread + 1)
    position = jnp.arange(name_count, dtype=jnp.int32)
    run_index = jnp.sum((position[:, None] >= cut_points[None, :]).astype(jnp.int32), axis=1)
    shuffle_score = jax.random.randint(key_list[2], (others,), 0, 1 << 20) * others + jnp.arange(others, dtype=jnp.int32)
    run_owner = jnp.argsort(shuffle_score).astype(jnp.int32)
    picked = run_owner[run_index]
    named_other = jnp.where(picked >= hot_expert, picked + 1, picked)
    in_hot = token_rank < CAP
    first_name = jnp.where(in_hot, hot_expert, named_other[:TOK_MB])
    second_at = jnp.where(in_hot, token_rank, TOK_MB + token_rank - CAP)
    second_name = named_other[second_at]
    flipped = jax.random.randint(key_list[3], (TOK_MB,), 0, 2) == 1
    paired = jnp.stack([jnp.where(flipped, second_name, first_name), jnp.where(flipped, first_name, second_name)], axis=1)
    inverse = jnp.argsort(token_order).astype(jnp.int32)
    return paired[inverse]


def draw_routes(key, part):
    block_total = SECTIONS * MB * OWNERS
    key_list = jax.random.split(jax.random.fold_in(key, 11), 4)
    free_hot = jax.random.randint(key_list[0], (SECTIONS, MB, OWNERS), 0, ROUTED)
    theme_expert = jax.random.randint(key_list[1], (SECTIONS, 1, 1), 0, EXPERTS)
    forced_batch = jax.random.randint(key_list[2], (SECTIONS, 1, 1), 0, MB)
    batch_rank = jnp.arange(MB, dtype=jnp.int32)[None, :, None]
    hot_expert = jnp.where(batch_rank == forced_batch, theme_expert, free_hot).reshape(block_total)
    block_keys = jax.random.split(key_list[3], block_total)
    paired = jax.vmap(route_block)(block_keys, hot_expert)
    return paired.reshape(SECTIONS, MB, OWNERS * TOK_MB, TOP).astype(jnp.int32)


def block_levels(rng, dims, pieces, low, high):
    def one(axis_at, parts):
        steps = jax.random.uniform(jax.random.fold_in(jax.random.fold_in(rng, 6), axis_at), (parts,), jnp.float32, low / len(pieces), high / len(pieces))
        return jnp.repeat(jnp.exp(steps), dims[axis_at] // parts).reshape((-1,) + (1,) * (len(dims) - axis_at - 1))

    level = one(*pieces[0])
    for cut in pieces[1:]:
        level = level * one(*cut)
    return level


def length_profile(count, total, reach, lean):
    portions = [(1 << 20) // math.isqrt(grade ** lean) + 1 for grade in range(2, count + 1)]
    surplus, counts = total - reach - (count - 1), [1] * (count - 1)
    while surplus > 0:
        candidates = [i for i in range(count - 1) if counts[i] < reach]
        mass, budget = sum([portions[i] for i in candidates]), surplus
        for i in candidates:
            more = min(reach - counts[i], max(1, budget * portions[i] // mass), surplus)
            counts[i] = counts[i] + more
            surplus = surplus - more
    return np.array([reach] + counts)


def ragged_sizes(key, number_of, total, bound, lean):
    if number_of == 2:
        one = jax.random.randint(key, (), max(1, total - bound), min(bound, total - 1) + 1)
        return jnp.stack([one, total - one])
    sizes = jnp.asarray(length_profile(number_of, total, bound, lean), jnp.int32)
    couples = (number_of - 1) // 2
    source_of, receiver = sizes[1:1 + 2 * couples:2], sizes[2:2 + 2 * couples:2]
    slack = jnp.minimum(source_of - 1, bound - receiver)
    shifted = jax.random.randint(jax.random.fold_in(key, 1), (couples,), 0, 1 << 20) % (slack + 1)
    sizes = sizes.at[1:1 + 2 * couples:2].set(source_of - shifted).at[2:2 + 2 * couples:2].set(receiver + shifted)
    return sizes[jax.random.permutation(jax.random.fold_in(key, 2), number_of)]


def gaussian(stream_key, dims, deviation, most, shards=(), held_as=jnp.bfloat16):
    result = deviation * jax.random.normal(stream_key, dims, jnp.float32)
    if shards:
        result = result * block_levels(stream_key, dims, shards, -0.22, 0.18)
    return jnp.clip(result, -most, most).astype(held_as)


def setup_inputs(seed: int = 0) -> dict:
    splits = jax.random.split(jax.random.key(seed), 9)
    routes = draw_routes(jax.random.fold_in(splits[8], 71), 0)
    route_probs = jnp.clip(0.2 + 0.8 * jax.random.uniform(splits[1], (SECTIONS, MB, TOKENS, TOP), jnp.float32) ** block_levels(splits[1], (SECTIONS, MB, TOKENS, TOP), ((0, 8), (2, 2)), -0.2, 0.2), 0.2, 1.0)
    example_ids = jax.vmap(lambda own: jnp.searchsorted(jnp.cumsum(ragged_sizes(own, SEQS, TOK_MB, LONGEST, 1)), jnp.arange(TOK_MB), side="right"))(jax.random.split(splits[2], MB * OWNERS)).reshape((MB, OWNERS, TOK_MB)).astype(jnp.int32)
    top_cotangent = gaussian(splits[3], (MB, TOKENS, D), 1.0, 6.0, ((1, 2), (2, 2)))
    branch_cotangent = gaussian(splits[4], (SECTIONS, MB, TOKENS, D), 0.5, 4.0, ((0, 8), (2, 2), (3, 2)))
    hidden_acts = gaussian(splits[5], (SECTIONS, EXPERTS, MB, SLOTS, FF), 1.0, 6.0, ((0, 8), (1, 2), (4, 2)))
    basis_hidden = gaussian(splits[6], (SECTIONS, EXPERTS, FF, KI), FF ** -0.5, 0.046875, ((0, 8), (1, 2), (2, 2)))
    basis_model = gaussian(splits[7], (SECTIONS, EXPERTS, D, KJ), D ** -0.5, 0.078125, ((0, 8), (1, 2), (2, 2)))
    return dict(routes=routes, route_probs=route_probs, example_ids=example_ids, top_cotangent=top_cotangent, branch_cotangent=branch_cotangent, hidden_acts=hidden_acts, basis_hidden=basis_hidden, basis_model=basis_model)


def dispatch_tables(route_rows, prob_rows, example_rows, experts, capacity):
    expert_hit = (route_rows[:, :, :, None] == jnp.arange(experts, dtype=jnp.int32)).astype(jnp.int32)
    expert_count = jnp.sum(expert_hit, axis=2)
    slot_rank = jnp.cumsum(expert_count, axis=1) - expert_count
    expert_prob = jnp.sum(expert_hit.astype(jnp.float32) * prob_rows[:, :, :, None], axis=2)
    slot_match = (slot_rank[:, :, :, None] == jnp.arange(capacity, dtype=jnp.int32)) & (expert_count[:, :, :, None] > 0)
    dispatch_weight = jnp.where(slot_match, expert_prob[:, :, :, None], jnp.float32(0.0))
    slot_example = jnp.sum(jnp.where(slot_match, example_rows[:, :, None, None] + 1, 0), axis=1) - 1
    return dispatch_weight, slot_example.astype(jnp.int32)


def example_squares(rotated_hidden, rotated_model, slot_example, examples):
    member = slot_example[:, None, :] == jnp.arange(examples, dtype=jnp.int32)[None, :, None]
    masked = jnp.where(member[:, :, :, None], rotated_hidden[:, None, :, :].astype(jnp.float32), jnp.float32(0.0))
    example_grad = jnp.einsum("osci,ocj->osij", masked, rotated_model.astype(jnp.float32))
    return jnp.sum(example_grad * example_grad, axis=(0, 1))


def reference(routes, route_probs, example_ids, top_cotangent, branch_cotangent, hidden_acts, basis_hidden, basis_model):
    owners = N_EXPERT
    branch_wide = branch_cotangent.astype(jnp.float32)
    suffix_sum = jnp.cumsum(branch_wide[::-1], axis=0)[::-1]
    later_all = jnp.concatenate([suffix_sum[1:], jnp.zeros_like(suffix_sum[:1])], axis=0)
    layer_list = []
    for layer_now in range(SECTIONS):
        cotangent = (top_cotangent.astype(jnp.float32) + later_all[layer_now]).reshape(MB * owners, TOK_MB, D)
        dispatch_weight, slot_example = dispatch_tables(
            routes[layer_now].reshape(MB * owners, TOK_MB, TOP),
            route_probs[layer_now].reshape(MB * owners, TOK_MB, TOP),
            example_ids.reshape(MB * owners, TOK_MB), EXPERTS, CAP)
        send_rows = jnp.einsum("ntec,ntd->necd", dispatch_weight, cotangent, precision=lax.Precision.HIGHEST).astype(jnp.bfloat16)
        send_rows = send_rows.reshape(MB, owners, EXPERTS, CAP, D)
        slot_example = slot_example.reshape(MB, owners, EXPERTS, CAP)
        expert_list = []
        for expert_now in range(EXPERTS):
            model_rows = send_rows[:, :, expert_now].astype(jnp.float32)
            rotated_model = jnp.einsum("mocd,dk->mock", model_rows, basis_model[layer_now, expert_now].astype(jnp.float32)).astype(jnp.bfloat16)
            rotated_hidden = jnp.einsum("msf,fk->msk", hidden_acts[layer_now, expert_now].astype(jnp.float32), basis_hidden[layer_now, expert_now].astype(jnp.float32)).astype(jnp.bfloat16)
            rotated_hidden = rotated_hidden.reshape(MB, owners, CAP, KI)
            square_sum = jnp.zeros((KI, KJ), jnp.float32)
            for micro_batch in range(MB):
                square_sum = square_sum + example_squares(rotated_hidden[micro_batch], rotated_model[micro_batch], slot_example[micro_batch, :, expert_now], SEQS)
            expert_list.append(square_sum / (MB * owners * SEQS))
        layer_list.append(jnp.stack(expert_list))
    return jnp.stack(layer_list)
```

```python
import functools

import jax
import jax.numpy as jnp
from jax import lax
from jax.experimental import pallas as pl
from jax.experimental.pallas import tpu as pltpu
from jax.sharding import PartitionSpec as P

SEQS = 2
MESH = pl.DeviceIdType.MESH


def kernel(
    sections,
    routes,
    probs,
    examples,
    top,
    branch,
    hidden,
    basis_hidden,
    basis_model,
    out,
    top_v,
    own_v,
    hidden_v,
    bh_v,
    bm_v,
    pair_in,
    chain_in,
    chain_out,
    swap_out,
    swap_in,
    select_v,
    prob_v,
    ex_out,
    ex_all,
    rows_out,
    rows_all,
    part_out,
    part_own,
    part_in,
    hid_own,
    hid_in,
    hid_sum,
    local_sem,
    pair_s,
    pair_r,
    chain_s,
    chain_r,
    swap_s,
    swap_r,
    rows_s,
    rows_r,
    part_s,
    part_r,
    one_s,
    one_r,
):
    batches, tokens, width = top.shape
    half = width // 2
    cap = rows_out.shape[2]
    section = lax.axis_index("section")
    core = lax.axis_index("expert")
    shard = lax.axis_index("shard")
    low = lax.rem(section, 2)
    high = section // 2
    last = sections // 2 - 1
    partner = {"section": section + 1 - 2 * low}
    other_core = {"expert": 1 - core}
    other_shard = {"shard": 1 - shard}
    cols = part_out.shape[2]
    pieces = bh_v.shape[0]
    depth = bh_v.shape[1]

    def columns(index):
        return pl.ds(pl.multiple_of(index * half, 128), half)

    loads = [
        pltpu.make_async_copy(branch.at[0, :, :, columns(low)], own_v, local_sem.at[0]),
        pltpu.make_async_copy(top.at[:, :, columns(0)], top_v.at[0], local_sem.at[1]),
        pltpu.make_async_copy(top.at[:, :, columns(1)], top_v.at[1], local_sem.at[2]),
        pltpu.make_async_copy(hidden.at[0, 0], hidden_v, local_sem.at[3]),
        pltpu.make_async_copy(
            basis_model.at[0, 0, :, pl.ds(0, cols)], bm_v.at[0], local_sem.at[4]
        ),
        pltpu.make_async_copy(
            basis_model.at[0, 0, :, pl.ds(cols, cols)], bm_v.at[1], local_sem.at[5]
        ),
    ]
    hidden_loads = [
        pltpu.make_async_copy(
            basis_hidden.at[0, 0, pl.ds(p * depth, depth)], bh_v.at[p], local_sem.at[6 + p]
        )
        for p in range(pieces)
    ]
    loads[0].start()
    loads[3].start()
    for load in hidden_loads:
        load.start()
    for index in (1, 2, 4, 5):
        loads[index].start()

    barrier = pltpu.get_barrier_semaphore()
    for target in (partner, other_core, other_shard):
        pl.semaphore_signal(barrier, inc=1, device_id=target, device_id_type=MESH)

    @pl.when(high > 0)
    def _():
        pl.semaphore_signal(
            barrier, inc=1, device_id={"section": section - 2}, device_id_type=MESH
        )

    @pl.when(high < last)
    def _():
        pl.semaphore_signal(
            barrier, inc=1, device_id={"section": section + 2}, device_id_type=MESH
        )

    pl.semaphore_wait(
        barrier, 3 + jnp.where(high > 0, 1, 0) + jnp.where(high < last, 1, 0)
    )

    def remote(source, target, send, receive, device):
        return pltpu.make_async_remote_copy(
            src_ref=source,
            dst_ref=target,
            send_sem=send,
            recv_sem=receive,
            device_id=device,
            device_id_type=MESH,
        )

    def pair_copy(m):
        return remote(
            branch.at[0, m, :, columns(1 - low)],
            pair_in.at[m],
            pair_s.at[m],
            pair_r.at[m],
            partner,
        )

    def chain_copy(m):
        return remote(
            chain_out.at[m], chain_in.at[m], chain_s.at[m], chain_r.at[m],
            {"section": section - 2},
        )

    def swap_copy(m):
        return remote(swap_out.at[m], swap_in.at[m], swap_s.at[m], swap_r.at[m], partner)

    def rows_copy(m):
        return remote(
            rows_out.at[m], rows_all.at[m, core], rows_s.at[m], rows_r.at[m], other_core
        )

    def part_copy(m):
        return remote(part_out.at[m], part_in.at[m], part_s.at[m], part_r.at[m], other_shard)

    ex_copy = remote(ex_out, ex_all.at[core], one_s.at[0], one_r.at[0], other_core)
    hid_copy = remote(hid_own, hid_in, one_s.at[1], one_r.at[1], other_shard)

    for m in range(batches):
        pair_copy(m).start()

    lane_token = lax.broadcasted_iota(jnp.int32, (tokens, tokens), 1)
    row_token = lax.broadcasted_iota(jnp.int32, (tokens, tokens), 0)
    slot_row = lax.broadcasted_iota(jnp.int32, (cap, tokens), 0).astype(jnp.float32)
    for m in range(batches):
        named = routes[0, m]
        weight = probs[0, m]
        example_row = examples[m].astype(jnp.float32)
        for place in range(2):
            expert = core if place == 0 else 1 - core
            hit = named == expert
            count = jnp.sum(jnp.where(hit, 1.0, 0.0), axis=1, keepdims=True)
            prob = jnp.sum(jnp.where(hit, weight, 0.0), axis=1, keepdims=True)
            rank_row = jnp.sum(
                jnp.where(row_token < lane_token, count, 0.0), axis=0, keepdims=True
            )
            count_row = jnp.sum(
                jnp.where(row_token == lane_token, count, 0.0), axis=0, keepdims=True
            )
            prob_row = jnp.sum(
                jnp.where(row_token == lane_token, prob, 0.0), axis=0, keepdims=True
            )
            match = jnp.where(slot_row == rank_row, 1.0, 0.0) * count_row
            slot_prob = jnp.sum(match * prob_row, axis=1, keepdims=True)
            slot_example = jnp.sum(match * (example_row + 1.0), axis=1, keepdims=True) - 1.0
            select_v[m, place * cap : (place + 1) * cap, :] = match.astype(jnp.bfloat16)
            prob_v[m, place * cap : (place + 1) * cap, :] = jnp.broadcast_to(
                slot_prob, (cap, prob_v.shape[2])
            )
            wide = jnp.broadcast_to(slot_example.astype(jnp.int32), (cap, ex_out.shape[2]))
            if place == 0:
                ex_all[core, m] = wide
            else:
                ex_out[m] = wide
    ex_copy.start()

    @pl.when(high == last)
    def _():
        chain_in[...] = jnp.zeros_like(chain_in)

    loads[0].wait()

    def carry(m):
        pair_copy(m).wait_recv()

        @pl.when(high < last)
        def _():
            chain_copy(m).wait_recv()

        own = own_v[m].astype(jnp.float32)
        before = chain_in[m].astype(jnp.float32)

        @pl.when(high > 0)
        def _():
            total = before + own + pair_in[m].astype(jnp.float32)
            chain_out[m] = total.astype(jnp.bfloat16)
            chain_copy(m).start()

        swap_out[m] = (before + jnp.where(low == 1, own, 0.0)).astype(jnp.bfloat16)
        swap_copy(m).start()

    def rotate_hidden():
        loads[3].wait()
        for p in range(pieces):
            hidden_loads[p].wait()
        hid_own[...] = jnp.zeros_like(hid_own)

        def piece(p, _):
            acts = hidden_v[:, :, pl.ds(pl.multiple_of(p * depth, 128), depth)]
            hid_own[...] += jnp.dot(
                acts.reshape(batches * acts.shape[1], depth),
                bh_v[p],
                preferred_element_type=jnp.float32,
            )
            return 0

        lax.fori_loop(0, pieces, piece, 0)
        hid_copy.start()

    def dispatch(m):
        swap_copy(m).wait_recv()
        select = select_v[m]
        pair_select = jnp.where(low == 0, select.astype(jnp.float32), 0.0).astype(jnp.bfloat16)
        slot_prob = prob_v[m][:, :1]

        def pick(matrix, rows):
            return jnp.dot(matrix, rows, preferred_element_type=jnp.float32)

        mine = pick(select, top_v[low, m]) + pick(select, chain_in[m])
        mine = (mine + pick(pair_select, pair_in[m])) * slot_prob
        rest = (pick(select, top_v[1 - low, m]) + pick(select, swap_in[m])) * slot_prob
        mine = mine.astype(jnp.bfloat16)
        rest = rest.astype(jnp.bfloat16)
        rows_out[m, low] = mine[cap:]
        rows_out[m, 1 - low] = rest[cap:]
        rows_copy(m).start()
        rows_all[m, core, low] = mine[:cap]
        rows_all[m, core, 1 - low] = rest[:cap]

    def rotate_model(m):
        rows_copy(m).wait_recv()

        def rotated(block):
            total = None
            for h in range(2):
                rows = jnp.concatenate([rows_all[m, 0, h], rows_all[m, 1, h]], axis=0)
                term = jnp.dot(
                    rows,
                    bm_v[block, h * half : (h + 1) * half, :],
                    preferred_element_type=jnp.float32,
                )
                total = term if total is None else total + term
            return total

        part_out[m] = rotated(1 - shard)
        part_copy(m).start()
        part_own[m] = rotated(shard)

    def squares(m):
        part_copy(m).wait_recv()
        model = (part_own[m] + part_in[m]).astype(jnp.bfloat16)
        hid = hid_sum[m]
        total = None
        for owner in range(2):
            block = hid[owner * cap : (owner + 1) * cap]
            ids = ex_all[owner, m][:, :1]
            for q in range(SEQS):
                masked = jnp.where(ids == q, block, 0.0).astype(jnp.bfloat16)
                grad = lax.dot_general(
                    masked,
                    model[owner * cap : (owner + 1) * cap],
                    (((0,), (0,)), ((), ())),
                    preferred_element_type=jnp.float32,
                )
                total = grad * grad if total is None else total + grad * grad
        out[0, 0] += total

    def step(k, _):
        @pl.when(k < batches)
        def _():
            carry(k)

        @pl.when(k == 0)
        def _():
            rotate_hidden()

        @pl.when(k == 1)
        def _():
            loads[1].wait()
            loads[2].wait()

        @pl.when(jnp.logical_and(k >= 1, k < batches + 1))
        def _():
            dispatch(k - 1)

        @pl.when(k == 2)
        def _():
            loads[4].wait()
            loads[5].wait()

        @pl.when(jnp.logical_and(k >= 2, k < batches + 2))
        def _():
            rotate_model(k - 2)

        @pl.when(k == 3)
        def _():
            ex_copy.wait_recv()
            hid_copy.wait_recv()
            hid = hid_own[...] + hid_in[...]
            hid_sum[...] = hid.reshape(hid_sum.shape)
            out[...] = jnp.zeros_like(out)

        @pl.when(k >= 3)
        def _():
            squares(k - 3)

        return 0

    lax.fori_loop(0, batches + 3, step, 0)
    out[...] = out[...] / (batches * 2 * SEQS)

    for m in range(batches):
        pair_copy(m).wait_send()
        swap_copy(m).wait_send()
        rows_copy(m).wait_send()
        part_copy(m).wait_send()
    ex_copy.wait_send()
    hid_copy.wait_send()

    @pl.when(high > 0)
    def _():
        for m in range(batches):
            chain_copy(m).wait_send()


def on_device(
    routes,
    route_probs,
    example_ids,
    top_cotangent,
    branch_cotangent,
    hidden_acts,
    basis_hidden,
    basis_model,
):
    sections = lax.axis_size("section")
    shards = lax.axis_size("shard")
    batches, tokens, width = top_cotangent.shape
    slots, depth = hidden_acts.shape[3:]
    cap = slots // lax.axis_size("expert")
    rank_hidden = basis_hidden.shape[3]
    cols = basis_model.shape[3] // shards
    half = width // 2
    pieces = 4
    bf16, f32 = jnp.bfloat16, jnp.float32
    vmem = pl.BlockSpec(memory_space=pltpu.VMEM)
    hbm = pl.BlockSpec(memory_space=pl.ANY)
    dma = pltpu.SemaphoreType.DMA
    chunk = (batches, tokens, half)
    flops = 2 * batches * slots * (depth * rank_hidden + width * cols * shards)
    return pl.pallas_call(
        functools.partial(kernel, sections),
        out_shape=jax.ShapeDtypeStruct((1, 1, rank_hidden, cols), f32),
        in_specs=[vmem] * 3 + [hbm] * 5,
        out_specs=vmem,
        scratch_shapes=[
            pltpu.VMEM((2,) + chunk, bf16),
            pltpu.VMEM(chunk, bf16),
            pltpu.VMEM((batches, slots, depth), bf16),
            pltpu.VMEM((pieces, depth // pieces, rank_hidden), bf16),
            pltpu.VMEM((2, width, cols), bf16),
            pltpu.VMEM(chunk, bf16),
            pltpu.VMEM(chunk, bf16),
            pltpu.VMEM(chunk, bf16),
            pltpu.VMEM(chunk, bf16),
            pltpu.VMEM(chunk, bf16),
            pltpu.VMEM((batches, 2 * cap, tokens), bf16),
            pltpu.VMEM((batches, 2 * cap, 128), f32),
            pltpu.VMEM((batches, cap, 128), jnp.int32),
            pltpu.VMEM((2, batches, cap, 128), jnp.int32),
            pltpu.VMEM((batches, 2, cap, half), bf16),
            pltpu.VMEM((batches, 2, 2, cap, half), bf16),
            pltpu.VMEM((batches, slots, cols), f32),
            pltpu.VMEM((batches, slots, cols), f32),
            pltpu.VMEM((batches, slots, cols), f32),
            pltpu.VMEM((batches * slots, rank_hidden), f32),
            pltpu.VMEM((batches * slots, rank_hidden), f32),
            pltpu.VMEM((batches, slots, rank_hidden), f32),
            dma((6 + pieces,)),
            dma((batches,)),
            dma((batches,)),
            dma((batches,)),
            dma((batches,)),
            dma((batches,)),
            dma((batches,)),
            dma((batches,)),
            dma((batches,)),
            dma((batches,)),
            dma((batches,)),
            dma((2,)),
            dma((2,)),
        ],
        compiler_params=pltpu.CompilerParams(
            collective_id=0, has_side_effects=True, vmem_limit_bytes=48 * 1024 * 1024
        ),
        cost_estimate=pl.CostEstimate(
            flops=flops, bytes_accessed=16 * 1024 * 1024, transcendentals=0
        ),
    )(
        routes,
        route_probs,
        example_ids,
        top_cotangent,
        branch_cotangent,
        hidden_acts,
        basis_hidden,
        basis_model,
    )


def solution(mesh):
    return jax.shard_map(
        on_device,
        mesh=mesh,
        in_specs=(
            P("section", None, "expert", None),
            P("section", None, "expert", None),
            P(None, "expert", None),
            P(None, "expert", "shard"),
            P("section", None, "expert", "shard"),
            P("section", "expert", None, None, "shard"),
            P("section", "expert", "shard", None),
            P("section", "expert", "shard", None),
        ),
        out_specs=P("section", "expert", None, "shard"),
        check_vma=False,
    )
```

```python
import functools

import jax
import jax.numpy as jnp
from jax import lax
from jax.experimental import pallas as pl
from jax.experimental.pallas import tpu as pltpu
from jax.sharding import PartitionSpec as P

SEQS = 2
CHUNK = 256
IN_FLIGHT = 3
MESH = pl.DeviceIdType.MESH


def kernel(
    sections,
    routes,
    probs,
    examples,
    top,
    branch,
    hidden,
    basis_hidden,
    basis_model,
    out,
    routes_v,
    probs_v,
    examples_v,
    top_v,
    own_v,
    hidden_v,
    bh_v,
    bm_v,
    pair_in,
    chain_in,
    chain_out,
    swap_out,
    swap_in,
    select_v,
    prob_v,
    ex_out,
    ex_all,
    rows_out,
    rows_all,
    model_sum,
    part_out,
    part_in,
    hid_own,
    hid_in,
    hid_t,
    local_sem,
    pair_s,
    pair_r,
    chain_s,
    chain_r,
    swap_s,
    swap_r,
    rows_s,
    rows_r,
    part_s,
    part_r,
    one_s,
    one_r,
):
    batches, tokens, width = top.shape
    half = width // 2
    chunks = pair_in.shape[0]
    chunk = pair_in.shape[3]
    cap = part_out.shape[2]
    rows = batches * cap
    flat = batches * tokens
    section = lax.axis_index("section")
    core = lax.axis_index("expert")
    shard = lax.axis_index("shard")
    low = lax.rem(section, 2)
    high = section // 2
    last = sections // 2 - 1
    partner = {"section": section + 1 - 2 * low}
    other_core = {"expert": 1 - core}
    other_shard = {"shard": 1 - shard}
    cols = part_out.shape[3]
    pieces = 4
    piece_depth = bh_v.shape[0] // pieces

    def columns(half_index, index):
        return pl.ds(pl.multiple_of(half_index * half + index * chunk, 128), chunk)

    small_loads = [
        pltpu.make_async_copy(source, target, local_sem.at[index])
        for index, (source, target) in enumerate(
            ((routes, routes_v), (probs, probs_v), (examples, examples_v))
        )
    ]
    own_load = pltpu.make_async_copy(
        branch.at[0, :, :, pl.ds(pl.multiple_of(low * half, 128), half)], own_v, local_sem.at[3]
    )
    hidden_load = pltpu.make_async_copy(hidden.at[0, 0], hidden_v, local_sem.at[4])
    top_load = pltpu.make_async_copy(top, top_v, local_sem.at[5])
    model_load = pltpu.make_async_copy(basis_model.at[0, 0], bm_v, local_sem.at[6])
    basis_load = pltpu.make_async_copy(basis_hidden.at[0, 0], bh_v, local_sem.at[7])
    for load in small_loads + [own_load]:
        load.start()

    barrier = pltpu.get_barrier_semaphore()
    for target in (partner, other_core, other_shard):
        pl.semaphore_signal(barrier, inc=1, device_id=target, device_id_type=MESH)

    @pl.when(high > 0)
    def _():
        pl.semaphore_signal(
            barrier, inc=1, device_id={"section": section - 2}, device_id_type=MESH
        )

    @pl.when(high < last)
    def _():
        pl.semaphore_signal(
            barrier, inc=1, device_id={"section": section + 2}, device_id_type=MESH
        )

    pl.semaphore_wait(
        barrier, 3 + jnp.where(high > 0, 1, 0) + jnp.where(high < last, 1, 0)
    )

    def remote(source, target, send, receive, device):
        return pltpu.make_async_remote_copy(
            src_ref=source,
            dst_ref=target,
            send_sem=send,
            recv_sem=receive,
            device_id=device,
            device_id_type=MESH,
        )

    def pair_copy(c):
        return remote(
            branch.at[0, :, :, columns(1 - low, c)],
            pair_in.at[c],
            pair_s.at[c],
            pair_r.at[c],
            partner,
        )

    def chain_copy(c):
        return remote(
            chain_out.at[c], chain_in.at[c], chain_s.at[c], chain_r.at[c],
            {"section": section - 2},
        )

    def swap_copy(c):
        return remote(swap_out.at[c], swap_in.at[c], swap_s.at[c], swap_r.at[c], partner)

    def rows_copy(c):
        return remote(
            rows_out.at[c], rows_all.at[core, c], rows_s.at[c], rows_r.at[c], other_core
        )

    def part_copy(m):
        return remote(part_out.at[m], part_in.at[m], part_s.at[m], part_r.at[m], other_shard)

    ex_copy = remote(ex_out, ex_all.at[core], one_s.at[0], one_r.at[0], other_core)
    hid_copy = remote(hid_own, hid_in, one_s.at[1], one_r.at[1], other_shard)

    for c in range(min(IN_FLIGHT, chunks)):
        pair_copy(c).start()
    hidden_load.start()
    basis_load.start()
    top_load.start()
    model_load.start()

    lane_token = lax.broadcasted_iota(jnp.int32, (tokens, tokens), 1)
    row_token = lax.broadcasted_iota(jnp.int32, (tokens, tokens), 0)
    slot_row = lax.broadcasted_iota(jnp.int32, (cap, tokens), 0).astype(jnp.float32)
    select_v[...] = jnp.zeros_like(select_v)
    for load in small_loads:
        load.wait()
    for m in range(batches):
        named = routes_v[0, m]
        weight = probs_v[0, m]
        example_row = examples_v[m].astype(jnp.float32)
        for place in range(2):
            expert = core if place == 0 else 1 - core
            hit = named == expert
            count_row = jnp.sum(jnp.where(hit, 1.0, 0.0), axis=0, keepdims=True)
            prob_row = jnp.sum(jnp.where(hit, weight, 0.0), axis=0, keepdims=True)
            count = jnp.sum(
                jnp.where(row_token == lane_token, count_row, 0.0), axis=1, keepdims=True
            )
            rank_row = jnp.sum(
                jnp.where(row_token < lane_token, count, 0.0), axis=0, keepdims=True
            )
            match = jnp.where(slot_row == rank_row, 1.0, 0.0) * count_row
            slot_prob = jnp.sum(match * prob_row, axis=1, keepdims=True)
            slot_example = jnp.sum(match * (example_row + 1.0), axis=1, keepdims=True) - 1.0
            first = place * rows + m * cap
            select_v[first : first + cap, m * tokens : (m + 1) * tokens] = match.astype(
                jnp.bfloat16
            )
            prob_v[first : first + cap, :] = jnp.broadcast_to(slot_prob, (cap, prob_v.shape[1]))
            wide = jnp.broadcast_to(slot_example.astype(jnp.int32), (cap, ex_out.shape[2]))
            if place == 0:
                ex_all[core, m] = wide
            else:
                ex_out[m] = wide
    ex_copy.start()

    @pl.when(high == last)
    def _():
        chain_in[...] = jnp.zeros_like(chain_in)

    own_load.wait()

    def feed(c):
        pair_copy(c).wait_send()

        @pl.when(c + IN_FLIGHT < chunks)
        def _():
            pair_copy(c + IN_FLIGHT).start()

    def carry(c):
        pair_copy(c).wait_recv()

        @pl.when(high < last)
        def _():
            chain_copy(c).wait_recv()

        own = own_v[:, :, pl.ds(pl.multiple_of(c * chunk, 128), chunk)].astype(jnp.float32)
        before = chain_in[c].astype(jnp.float32)

        @pl.when(high > 0)
        def _():
            total = before + own + pair_in[c].astype(jnp.float32)
            chain_out[c] = total.astype(jnp.bfloat16)
            chain_copy(c).start()

        swap_out[c] = (before + jnp.where(low == 1, own, 0.0)).astype(jnp.bfloat16)
        swap_copy(c).start()

    def rotate_hidden():
        hidden_load.wait()
        basis_load.wait()
        hid_own[...] = jnp.zeros_like(hid_own)

        def piece(p, _):
            acts = hidden_v[:, :, pl.ds(pl.multiple_of(p * piece_depth, 128), piece_depth)]
            hid_own[...] += jnp.dot(
                acts.reshape(batches * acts.shape[1], piece_depth),
                bh_v[pl.ds(pl.multiple_of(p * piece_depth, 128), piece_depth), :],
                preferred_element_type=jnp.float32,
            )
            return 0

        lax.fori_loop(0, pieces, piece, 0)
        hid_copy.start()

    def dispatch(c):
        swap_copy(c).wait_recv()
        select = select_v[...]
        pair_select = jnp.where(low == 0, select.astype(jnp.float32), 0.0).astype(jnp.bfloat16)
        slot_prob = prob_v[:, :1]

        def pick(matrix, block):
            return jnp.dot(
                matrix, block.reshape(flat, chunk), preferred_element_type=jnp.float32
            )

        mine = pick(select, top_v[:, :, columns(low, c)]) + pick(select, chain_in[c])
        mine = (mine + pick(pair_select, pair_in[c])) * slot_prob
        rest = pick(select, top_v[:, :, columns(1 - low, c)]) + pick(select, swap_in[c])
        rest = rest * slot_prob
        mine = mine.astype(jnp.bfloat16)
        rest = rest.astype(jnp.bfloat16)
        rows_out[c, low] = mine[rows:]
        rows_out[c, 1 - low] = rest[rows:]
        rows_copy(c).start()
        rows_all[core, c, low] = mine[:rows]
        rows_all[core, c, 1 - low] = rest[:rows]

    def rotate_model(c):
        rows_copy(c).wait_recv()
        total = None
        for h in range(2):
            term = jnp.dot(
                jnp.concatenate([rows_all[0, c, h], rows_all[1, c, h]], axis=0),
                bm_v[pl.ds(pl.multiple_of(h * half + c * chunk, 128), chunk), :],
                preferred_element_type=jnp.float32,
            )
            total = term if total is None else total + term

        @pl.when(c == 0)
        def _():
            model_sum[...] = total

        @pl.when(c > 0)
        def _():
            model_sum[...] += total

    def block_columns(index):
        return pl.ds(pl.multiple_of(index * cols, 128), cols)

    def squares(m):
        part_copy(m).wait_recv()
        blocks = []
        for owner in range(2):
            first = pl.ds(pl.multiple_of(owner * rows + m * cap, 16), cap)
            blocks.append(
                model_sum[first, block_columns(shard)]
                + part_in[m, owner].astype(jnp.float32)
            )
        total = None
        for owner in range(2):
            ids = ex_all[owner, m][:, :1]
            for q in range(SEQS):
                kept = jnp.where(ids == q, blocks[owner], 0.0)
                empty = jnp.zeros_like(kept)
                both = [kept, empty] if owner == 0 else [empty, kept]
                grad = jnp.dot(
                    hid_t[m],
                    jnp.concatenate(both, axis=0).astype(jnp.bfloat16),
                    preferred_element_type=jnp.float32,
                )
                total = grad * grad if total is None else total + grad * grad

        @pl.when(m == 0)
        def _():
            out[0, 0] = total

        @pl.when(m > 0)
        def _():
            out[0, 0] += total

    early = high < last - 1
    lag = jnp.minimum(chunks, 1 + 2 * high)

    @pl.when(high < last)
    def _():
        lax.fori_loop(0, chunks, lambda c, _: (feed(c), 0)[1], 0)

    @pl.when(early)
    def _():
        rotate_hidden()

    def step(k, _):
        @pl.when(k < chunks)
        def _():
            carry(k)

            @pl.when(high == last)
            def _():
                feed(k)

        @pl.when(jnp.logical_and(k == chunks - 1, jnp.logical_not(early)))
        def _():
            rotate_hidden()

        @pl.when(k == lag)
        def _():
            top_load.wait()
            model_load.wait()

        @pl.when(jnp.logical_and(k >= lag, k < chunks + lag))
        def _():
            dispatch(k - lag)

        @pl.when(k >= lag + 1)
        def _():
            rotate_model(k - lag - 1)

        return 0

    lax.fori_loop(0, chunks + lag + 1, step, 0)

    for m in range(batches):
        for owner in range(2):
            first = owner * rows + m * cap
            part_out[m, owner] = model_sum[
                first : first + cap, block_columns(1 - shard)
            ].astype(jnp.bfloat16)
        part_copy(m).start()
    ex_copy.wait_recv()
    hid_copy.wait_recv()
    turned = (hid_own[...] + hid_in[...]).T
    for m in range(batches):
        hid_t[m] = turned[:, 2 * m * cap : 2 * (m + 1) * cap].astype(jnp.bfloat16)
    lax.fori_loop(0, batches, lambda m, _: (squares(m), 0)[1], 0)
    out[...] = out[...] / (batches * 2 * SEQS)

    for c in range(chunks):
        swap_copy(c).wait_send()
        rows_copy(c).wait_send()
    for m in range(batches):
        part_copy(m).wait_send()
    ex_copy.wait_send()
    hid_copy.wait_send()

    @pl.when(high > 0)
    def _():
        for c in range(chunks):
            chain_copy(c).wait_send()


def on_device(
    routes,
    route_probs,
    example_ids,
    top_cotangent,
    branch_cotangent,
    hidden_acts,
    basis_hidden,
    basis_model,
):
    sections = lax.axis_size("section")
    shards = lax.axis_size("shard")
    batches, tokens, width = top_cotangent.shape
    slots, depth = hidden_acts.shape[3:]
    cap = slots // lax.axis_size("expert")
    rank_hidden = basis_hidden.shape[3]
    cols = basis_model.shape[3] // shards
    half = width // 2
    chunk = CHUNK if half % CHUNK == 0 else 128
    chunks = half // chunk
    bf16, f32 = jnp.bfloat16, jnp.float32
    vmem = pl.BlockSpec(memory_space=pltpu.VMEM)
    hbm = pl.BlockSpec(memory_space=pl.ANY)
    dma = pltpu.SemaphoreType.DMA
    moving = pltpu.VMEM((chunks, batches, tokens, chunk), bf16)
    routes = jnp.swapaxes(routes, 2, 3)
    route_probs = jnp.swapaxes(route_probs, 2, 3)
    flops = 2 * batches * slots * (depth * rank_hidden + width * cols * shards)
    return pl.pallas_call(
        functools.partial(kernel, sections),
        out_shape=jax.ShapeDtypeStruct((1, 1, rank_hidden, cols), f32),
        in_specs=[hbm] * 8,
        out_specs=vmem,
        scratch_shapes=[
            pltpu.VMEM(routes.shape, jnp.int32),
            pltpu.VMEM(route_probs.shape, f32),
            pltpu.VMEM(example_ids.shape, jnp.int32),
            pltpu.VMEM((batches, tokens, width), bf16),
            pltpu.VMEM((batches, tokens, half), bf16),
            pltpu.VMEM((batches, slots, depth), bf16),
            pltpu.VMEM((depth, rank_hidden), bf16),
            pltpu.VMEM((width, cols * shards), bf16),
            moving,
            moving,
            moving,
            moving,
            moving,
            pltpu.VMEM((2 * batches * cap, batches * tokens), bf16),
            pltpu.VMEM((2 * batches * cap, 128), f32),
            pltpu.VMEM((batches, cap, 128), jnp.int32),
            pltpu.VMEM((2, batches, cap, 128), jnp.int32),
            pltpu.VMEM((chunks, 2, batches * cap, chunk), bf16),
            pltpu.VMEM((2, chunks, 2, batches * cap, chunk), bf16),
            pltpu.VMEM((batches * slots, cols * shards), f32),
            pltpu.VMEM((batches, 2, cap, cols), bf16),
            pltpu.VMEM((batches, 2, cap, cols), bf16),
            pltpu.VMEM((batches * slots, rank_hidden), f32),
            pltpu.VMEM((batches * slots, rank_hidden), f32),
            pltpu.VMEM((batches, rank_hidden, slots), bf16),
            dma((8,)),
        ]
        + [dma((chunks,))] * 8
        + [dma((batches,))] * 2
        + [dma((2,))] * 2,
        compiler_params=pltpu.CompilerParams(
            collective_id=0, has_side_effects=True, vmem_limit_bytes=60 * 1024 * 1024
        ),
        cost_estimate=pl.CostEstimate(
            flops=flops, bytes_accessed=16 * 1024 * 1024, transcendentals=0
        ),
    )(
        routes,
        route_probs,
        example_ids,
        top_cotangent,
        branch_cotangent,
        hidden_acts,
        basis_hidden,
        basis_model,
    )


def solution(mesh):
    return jax.shard_map(
        on_device,
        mesh=mesh,
        in_specs=(
            P("section", None, "expert", None),
            P("section", None, "expert", None),
            P(None, "expert", None),
            P(None, "expert", "shard"),
            P("section", None, "expert", "shard"),
            P("section", "expert", None, None, "shard"),
            P("section", "expert", "shard", None),
            P("section", "expert", "shard", None),
        ),
        out_specs=P("section", "expert", None, "shard"),
        check_vma=False,
    )
```

```python
import functools

import jax
import jax.numpy as jnp
from jax import lax
from jax.experimental import pallas as pl
from jax.experimental.pallas import tpu as pltpu
from jax.sharding import PartitionSpec as P

SEQS = 2
CHUNK = 256
IN_FLIGHT = 3
SWAP_LAG = 2
ROWS_LAG = 2
HOP_LAG = 2
MESH = pl.DeviceIdType.MESH


def kernel(
    sections,
    routes,
    probs,
    examples,
    top,
    branch,
    hidden,
    basis_hidden,
    basis_model,
    out,
    routes_v,
    probs_v,
    examples_v,
    top_v,
    own_v,
    hidden_v,
    bh_v,
    bm_v,
    pair_in,
    chain_in,
    chain_out,
    swap_out,
    swap_in,
    select_v,
    prob_v,
    ex_out,
    ex_all,
    rows_out,
    rows_all,
    model_sum,
    part_out,
    part_in,
    hid_own,
    hid_in,
    hid_t,
    local_sem,
    pair_s,
    pair_r,
    chain_s,
    chain_r,
    swap_s,
    swap_r,
    rows_s,
    rows_r,
    part_s,
    part_r,
    one_s,
    one_r,
):
    batches, tokens, width = top.shape
    half = width // 2
    chunks = pair_in.shape[0]
    chunk = pair_in.shape[3]
    cap = part_out.shape[2]
    rows = batches * cap
    flat = batches * tokens
    section = lax.axis_index("section")
    core = lax.axis_index("expert")
    shard = lax.axis_index("shard")
    low = lax.rem(section, 2)
    high = section // 2
    last = sections // 2 - 1
    partner = {"section": section + 1 - 2 * low}
    other_core = {"expert": 1 - core}
    other_shard = {"shard": 1 - shard}
    cols = part_out.shape[3]
    pieces = 4
    piece_depth = bh_v.shape[0] // pieces

    def columns(half_index, index):
        return pl.ds(pl.multiple_of(half_index * half + index * chunk, 128), chunk)

    small_loads = [
        pltpu.make_async_copy(source, target, local_sem.at[index])
        for index, (source, target) in enumerate(
            ((routes, routes_v), (probs, probs_v), (examples, examples_v))
        )
    ]
    own_load = pltpu.make_async_copy(
        branch.at[0, :, :, pl.ds(pl.multiple_of(low * half, 128), half)], own_v, local_sem.at[3]
    )
    hidden_load = pltpu.make_async_copy(hidden.at[0, 0], hidden_v, local_sem.at[4])
    top_load = pltpu.make_async_copy(top, top_v, local_sem.at[5])
    model_load = pltpu.make_async_copy(basis_model.at[0, 0], bm_v, local_sem.at[6])
    basis_load = pltpu.make_async_copy(basis_hidden.at[0, 0], bh_v, local_sem.at[7])
    for load in small_loads + [own_load]:
        load.start()

    barrier = pltpu.get_barrier_semaphore()
    for target in (partner, other_core, other_shard):
        pl.semaphore_signal(barrier, inc=1, device_id=target, device_id_type=MESH)

    @pl.when(high > 0)
    def _():
        pl.semaphore_signal(
            barrier, inc=1, device_id={"section": section - 2}, device_id_type=MESH
        )

    @pl.when(high < last)
    def _():
        pl.semaphore_signal(
            barrier, inc=1, device_id={"section": section + 2}, device_id_type=MESH
        )

    pl.semaphore_wait(
        barrier, 3 + jnp.where(high > 0, 1, 0) + jnp.where(high < last, 1, 0)
    )

    def remote(source, target, send, receive, device):
        return pltpu.make_async_remote_copy(
            src_ref=source,
            dst_ref=target,
            send_sem=send,
            recv_sem=receive,
            device_id=device,
            device_id_type=MESH,
        )

    def pair_copy(c):
        return remote(
            branch.at[0, :, :, columns(1 - low, c)],
            pair_in.at[c],
            pair_s.at[c],
            pair_r.at[c],
            partner,
        )

    def chain_copy(c):
        return remote(
            chain_out.at[c], chain_in.at[c], chain_s.at[c], chain_r.at[c],
            {"section": section - 2},
        )

    def swap_copy(c):
        return remote(swap_out.at[c], swap_in.at[c], swap_s.at[c], swap_r.at[c], partner)

    def rows_copy(c):
        return remote(
            rows_out.at[c], rows_all.at[core, c], rows_s.at[c], rows_r.at[c], other_core
        )

    def part_copy(m):
        return remote(part_out.at[m], part_in.at[m], part_s.at[m], part_r.at[m], other_shard)

    ex_copy = remote(ex_out, ex_all.at[core], one_s.at[0], one_r.at[0], other_core)
    hid_copy = remote(hid_own, hid_in, one_s.at[1], one_r.at[1], other_shard)

    for c in range(min(IN_FLIGHT, chunks)):
        pair_copy(c).start()
    hidden_load.start()
    basis_load.start()
    top_load.start()
    model_load.start()

    lane_token = lax.broadcasted_iota(jnp.int32, (tokens, tokens), 1)
    row_token = lax.broadcasted_iota(jnp.int32, (tokens, tokens), 0)
    slot_row = lax.broadcasted_iota(jnp.int32, (cap, tokens), 0).astype(jnp.float32)
    select_v[...] = jnp.zeros_like(select_v)
    for load in small_loads:
        load.wait()
    for m in range(batches):
        named = routes_v[0, m]
        weight = probs_v[0, m]
        example_row = examples_v[m].astype(jnp.float32)
        for place in range(2):
            expert = core if place == 0 else 1 - core
            hit = named == expert
            count_row = jnp.sum(jnp.where(hit, 1.0, 0.0), axis=0, keepdims=True)
            prob_row = jnp.sum(jnp.where(hit, weight, 0.0), axis=0, keepdims=True)
            count = jnp.sum(
                jnp.where(row_token == lane_token, count_row, 0.0), axis=1, keepdims=True
            )
            rank_row = jnp.sum(
                jnp.where(row_token < lane_token, count, 0.0), axis=0, keepdims=True
            )
            match = jnp.where(slot_row == rank_row, 1.0, 0.0) * count_row
            slot_prob = jnp.sum(match * prob_row, axis=1, keepdims=True)
            slot_example = jnp.sum(match * (example_row + 1.0), axis=1, keepdims=True) - 1.0
            first = place * rows + m * cap
            select_v[first : first + cap, m * tokens : (m + 1) * tokens] = match.astype(
                jnp.bfloat16
            )
            prob_v[first : first + cap, :] = jnp.broadcast_to(slot_prob, (cap, prob_v.shape[1]))
            wide = jnp.broadcast_to(slot_example.astype(jnp.int32), (cap, ex_out.shape[2]))
            if place == 0:
                ex_all[core, m] = wide
            else:
                ex_out[m] = wide
    ex_copy.start()

    @pl.when(high == last)
    def _():
        chain_in[...] = jnp.zeros_like(chain_in)

    own_load.wait()

    def feed(c):
        pair_copy(c).wait_send()

        @pl.when(c + IN_FLIGHT < chunks)
        def _():
            pair_copy(c + IN_FLIGHT).start()

    def carry(c):
        pair_copy(c).wait_recv()

        @pl.when(high < last)
        def _():
            chain_copy(c).wait_recv()

        own = own_v[:, :, pl.ds(pl.multiple_of(c * chunk, 128), chunk)].astype(jnp.float32)
        before = chain_in[c].astype(jnp.float32)

        @pl.when(high > 0)
        def _():
            total = before + own + pair_in[c].astype(jnp.float32)
            chain_out[c] = total.astype(jnp.bfloat16)
            chain_copy(c).start()

        swap_out[c] = (before + jnp.where(low == 1, own, 0.0)).astype(jnp.bfloat16)

    def rotate_hidden():
        hidden_load.wait()
        basis_load.wait()
        hid_own[...] = jnp.zeros_like(hid_own)

        def piece(p, _):
            acts = hidden_v[:, :, pl.ds(pl.multiple_of(p * piece_depth, 128), piece_depth)]
            hid_own[...] += jnp.dot(
                acts.reshape(batches * acts.shape[1], piece_depth),
                bh_v[pl.ds(pl.multiple_of(p * piece_depth, 128), piece_depth), :],
                preferred_element_type=jnp.float32,
            )
            return 0

        lax.fori_loop(0, pieces, piece, 0)
        hid_copy.start()

    def dispatch(c):
        swap_copy(c).wait_recv()
        select = select_v[...]
        pair_select = jnp.where(low == 0, select.astype(jnp.float32), 0.0).astype(jnp.bfloat16)
        slot_prob = prob_v[:, :1]

        def pick(matrix, block):
            return jnp.dot(
                matrix, block.reshape(flat, chunk), preferred_element_type=jnp.float32
            )

        mine = pick(select, top_v[:, :, columns(low, c)]) + pick(select, chain_in[c])
        mine = (mine + pick(pair_select, pair_in[c])) * slot_prob
        rest = pick(select, top_v[:, :, columns(1 - low, c)]) + pick(select, swap_in[c])
        rest = rest * slot_prob
        mine = mine.astype(jnp.bfloat16)
        rest = rest.astype(jnp.bfloat16)
        rows_out[c, low] = mine[rows:]
        rows_out[c, 1 - low] = rest[rows:]
        rows_copy(c).start()
        rows_all[core, c, low] = mine[:rows]
        rows_all[core, c, 1 - low] = rest[:rows]

    def rotate_model(c):
        rows_copy(c).wait_recv()
        total = None
        for h in range(2):
            term = jnp.dot(
                jnp.concatenate([rows_all[0, c, h], rows_all[1, c, h]], axis=0),
                bm_v[pl.ds(pl.multiple_of(h * half + c * chunk, 128), chunk), :],
                preferred_element_type=jnp.float32,
            )
            total = term if total is None else total + term

        @pl.when(c == 0)
        def _():
            model_sum[...] = total

        @pl.when(c > 0)
        def _():
            model_sum[...] += total

    def block_columns(index):
        return pl.ds(pl.multiple_of(index * cols, 128), cols)

    def squares(m):
        part_copy(m).wait_recv()
        blocks = []
        for owner in range(2):
            first = pl.ds(pl.multiple_of(owner * rows + m * cap, 16), cap)
            blocks.append(
                model_sum[first, block_columns(shard)]
                + part_in[m, owner].astype(jnp.float32)
            )
        total = None
        for owner in range(2):
            ids = ex_all[owner, m][:, :1]
            for q in range(SEQS):
                kept = jnp.where(ids == q, blocks[owner], 0.0)
                empty = jnp.zeros_like(kept)
                both = [kept, empty] if owner == 0 else [empty, kept]
                grad = jnp.dot(
                    hid_t[m],
                    jnp.concatenate(both, axis=0).astype(jnp.bfloat16),
                    preferred_element_type=jnp.float32,
                )
                total = grad * grad if total is None else total + grad * grad

        @pl.when(m == 0)
        def _():
            out[0, 0] = total

        @pl.when(m > 0)
        def _():
            out[0, 0] += total

    early = high < last - 1
    held = jnp.minimum(chunks - 1, HOP_LAG * high)
    lag = held + SWAP_LAG
    model_lag = lag + ROWS_LAG

    @pl.when(high < last)
    def _():
        lax.fori_loop(0, chunks, lambda c, _: (feed(c), 0)[1], 0)

    @pl.when(early)
    def _():
        rotate_hidden()

    def step(k, _):
        @pl.when(k < chunks)
        def _():
            carry(k)

            @pl.when(high == last)
            def _():
                feed(k)

        @pl.when(jnp.logical_and(k == chunks - 1, jnp.logical_not(early)))
        def _():
            rotate_hidden()

        @pl.when(jnp.logical_and(k >= held, k < chunks + held))
        def _():
            swap_copy(k - held).start()

        @pl.when(k == lag)
        def _():
            top_load.wait()
            model_load.wait()

        @pl.when(jnp.logical_and(k >= lag, k < chunks + lag))
        def _():
            dispatch(k - lag)

        @pl.when(k >= model_lag)
        def _():
            rotate_model(k - model_lag)

        return 0

    lax.fori_loop(0, chunks + model_lag, step, 0)

    for m in range(batches):
        for owner in range(2):
            first = owner * rows + m * cap
            part_out[m, owner] = model_sum[
                first : first + cap, block_columns(1 - shard)
            ].astype(jnp.bfloat16)
        part_copy(m).start()
    ex_copy.wait_recv()
    hid_copy.wait_recv()
    turned = (hid_own[...] + hid_in[...]).T
    for m in range(batches):
        hid_t[m] = turned[:, 2 * m * cap : 2 * (m + 1) * cap].astype(jnp.bfloat16)
    lax.fori_loop(0, batches, lambda m, _: (squares(m), 0)[1], 0)

    for c in range(chunks):
        swap_copy(c).wait_send()
        rows_copy(c).wait_send()
    for m in range(batches):
        part_copy(m).wait_send()
    ex_copy.wait_send()
    hid_copy.wait_send()

    @pl.when(high > 0)
    def _():
        for c in range(chunks):
            chain_copy(c).wait_send()


def on_device(
    routes,
    route_probs,
    example_ids,
    top_cotangent,
    branch_cotangent,
    hidden_acts,
    basis_hidden,
    basis_model,
):
    sections = lax.axis_size("section")
    shards = lax.axis_size("shard")
    batches, tokens, width = top_cotangent.shape
    slots, depth = hidden_acts.shape[3:]
    cap = slots // lax.axis_size("expert")
    rank_hidden = basis_hidden.shape[3]
    cols = basis_model.shape[3] // shards
    half = width // 2
    chunk = CHUNK if half % CHUNK == 0 else 128
    chunks = half // chunk
    bf16, f32 = jnp.bfloat16, jnp.float32
    vmem = pl.BlockSpec(memory_space=pltpu.VMEM)
    hbm = pl.BlockSpec(memory_space=pl.ANY)
    dma = pltpu.SemaphoreType.DMA
    moving = pltpu.VMEM((chunks, batches, tokens, chunk), bf16)
    routes = jnp.swapaxes(routes, 2, 3)
    route_probs = jnp.swapaxes(route_probs, 2, 3)
    flops = 2 * batches * slots * (depth * rank_hidden + width * cols * shards)
    square_sum = pl.pallas_call(
        functools.partial(kernel, sections),
        out_shape=jax.ShapeDtypeStruct((1, 1, rank_hidden, cols), f32),
        in_specs=[hbm] * 8,
        out_specs=vmem,
        scratch_shapes=[
            pltpu.VMEM(routes.shape, jnp.int32),
            pltpu.VMEM(route_probs.shape, f32),
            pltpu.VMEM(example_ids.shape, jnp.int32),
            pltpu.VMEM((batches, tokens, width), bf16),
            pltpu.VMEM((batches, tokens, half), bf16),
            pltpu.VMEM((batches, slots, depth), bf16),
            pltpu.VMEM((depth, rank_hidden), bf16),
            pltpu.VMEM((width, cols * shards), bf16),
            moving,
            moving,
            moving,
            moving,
            moving,
            pltpu.VMEM((2 * batches * cap, batches * tokens), bf16),
            pltpu.VMEM((2 * batches * cap, 128), f32),
            pltpu.VMEM((batches, cap, 128), jnp.int32),
            pltpu.VMEM((2, batches, cap, 128), jnp.int32),
            pltpu.VMEM((chunks, 2, batches * cap, chunk), bf16),
            pltpu.VMEM((2, chunks, 2, batches * cap, chunk), bf16),
            pltpu.VMEM((batches * slots, cols * shards), f32),
            pltpu.VMEM((batches, 2, cap, cols), bf16),
            pltpu.VMEM((batches, 2, cap, cols), bf16),
            pltpu.VMEM((batches * slots, rank_hidden), f32),
            pltpu.VMEM((batches * slots, rank_hidden), f32),
            pltpu.VMEM((batches, rank_hidden, slots), bf16),
            dma((8,)),
        ]
        + [dma((chunks,))] * 8
        + [dma((batches,))] * 2
        + [dma((2,))] * 2,
        compiler_params=pltpu.CompilerParams(
            collective_id=0, has_side_effects=True, vmem_limit_bytes=60 * 1024 * 1024
        ),
        cost_estimate=pl.CostEstimate(
            flops=flops, bytes_accessed=16 * 1024 * 1024, transcendentals=0
        ),
    )(
        routes,
        route_probs,
        example_ids,
        top_cotangent,
        branch_cotangent,
        hidden_acts,
        basis_hidden,
        basis_model,
    )
    return square_sum / (batches * lax.axis_size("expert") * SEQS)


def solution(mesh):
    return jax.shard_map(
        on_device,
        mesh=mesh,
        in_specs=(
            P("section", None, "expert", None),
            P("section", None, "expert", None),
            P(None, "expert", None),
            P(None, "expert", "shard"),
            P("section", None, "expert", "shard"),
            P("section", "expert", None, None, "shard"),
            P("section", "expert", "shard", None),
            P("section", "expert", "shard", None),
        ),
        out_specs=P("section", "expert", None, "shard"),
        check_vma=False,
    )
```

```python
import functools

import jax
import jax.numpy as jnp
from jax import lax
from jax.experimental import pallas as pl
from jax.experimental.pallas import tpu as pltpu
from jax.sharding import PartitionSpec as P

SEQS = 2
CHUNK = 256
IN_FLIGHT = 3
SWAP_LAG = 2
ROWS_LAG = 2
HOP_LAG = 2
MESH = pl.DeviceIdType.MESH


def kernel(
    sections,
    routes,
    probs,
    examples,
    top,
    branch,
    hidden,
    basis_hidden,
    basis_model,
    out,
    routes_v,
    probs_v,
    examples_v,
    top_v,
    own_v,
    hidden_v,
    bh_v,
    bm_v,
    pair_in,
    chain_in,
    chain_out,
    swap_out,
    swap_in,
    select_v,
    prob_v,
    ex_out,
    ex_all,
    rows_out,
    rows_all,
    model_sum,
    part_out,
    part_in,
    hid_own,
    hid_in,
    hid_t,
    local_sem,
    pair_s,
    pair_r,
    chain_s,
    chain_r,
    swap_s,
    swap_r,
    rows_s,
    rows_r,
    part_s,
    part_r,
    one_s,
    one_r,
):
    batches, tokens, width = top.shape
    half = width // 2
    chunks = pair_in.shape[0]
    chunk = pair_in.shape[3]
    cap = part_out.shape[2]
    rows = batches * cap
    flat = batches * tokens
    section = lax.axis_index("section")
    core = lax.axis_index("expert")
    shard = lax.axis_index("shard")
    low = lax.rem(section, 2)
    high = section // 2
    last = sections // 2 - 1
    partner = {"section": section + 1 - 2 * low}
    other_core = {"expert": 1 - core}
    other_shard = {"shard": 1 - shard}
    cols = part_out.shape[3]
    pieces = 4
    piece_depth = bh_v.shape[0] // pieces
    group = batches // hid_t.shape[0]

    def columns(half_index, index):
        return pl.ds(pl.multiple_of(half_index * half + index * chunk, 128), chunk)

    small_loads = [
        pltpu.make_async_copy(source, target, local_sem.at[index])
        for index, (source, target) in enumerate(
            ((routes, routes_v), (probs, probs_v), (examples, examples_v))
        )
    ]
    own_load = pltpu.make_async_copy(
        branch.at[0, :, :, pl.ds(pl.multiple_of(low * half, 128), half)], own_v, local_sem.at[3]
    )
    hidden_load = pltpu.make_async_copy(hidden.at[0, 0], hidden_v, local_sem.at[4])
    top_load = pltpu.make_async_copy(top, top_v, local_sem.at[5])
    model_load = pltpu.make_async_copy(basis_model.at[0, 0], bm_v, local_sem.at[6])
    basis_load = pltpu.make_async_copy(basis_hidden.at[0, 0], bh_v, local_sem.at[7])
    for load in small_loads + [own_load]:
        load.start()

    barrier = pltpu.get_barrier_semaphore()
    for target in (partner, other_core, other_shard):
        pl.semaphore_signal(barrier, inc=1, device_id=target, device_id_type=MESH)

    @pl.when(high > 0)
    def _():
        pl.semaphore_signal(
            barrier, inc=1, device_id={"section": section - 2}, device_id_type=MESH
        )

    @pl.when(high < last)
    def _():
        pl.semaphore_signal(
            barrier, inc=1, device_id={"section": section + 2}, device_id_type=MESH
        )

    pl.semaphore_wait(
        barrier, 3 + jnp.where(high > 0, 1, 0) + jnp.where(high < last, 1, 0)
    )

    def remote(source, target, send, receive, device):
        return pltpu.make_async_remote_copy(
            src_ref=source,
            dst_ref=target,
            send_sem=send,
            recv_sem=receive,
            device_id=device,
            device_id_type=MESH,
        )

    def pair_copy(c):
        return remote(
            branch.at[0, :, :, columns(1 - low, c)],
            pair_in.at[c],
            pair_s.at[c],
            pair_r.at[c],
            partner,
        )

    def chain_copy(c):
        return remote(
            chain_out.at[c], chain_in.at[c], chain_s.at[c], chain_r.at[c],
            {"section": section - 2},
        )

    def swap_copy(c):
        return remote(swap_out.at[c], swap_in.at[c], swap_s.at[c], swap_r.at[c], partner)

    def rows_copy(c):
        return remote(
            rows_out.at[c], rows_all.at[core, c], rows_s.at[c], rows_r.at[c], other_core
        )

    def part_copy(m):
        return remote(part_out.at[m], part_in.at[m], part_s.at[m], part_r.at[m], other_shard)

    ex_copy = remote(ex_out, ex_all.at[core], one_s.at[0], one_r.at[0], other_core)
    hid_copy = remote(hid_own, hid_in, one_s.at[1], one_r.at[1], other_shard)

    for c in range(min(IN_FLIGHT, chunks)):
        pair_copy(c).start()
    hidden_load.start()
    basis_load.start()
    top_load.start()
    model_load.start()

    lane_token = lax.broadcasted_iota(jnp.int32, (tokens, tokens), 1)
    row_token = lax.broadcasted_iota(jnp.int32, (tokens, tokens), 0)
    slot_row = lax.broadcasted_iota(jnp.int32, (cap, tokens), 0).astype(jnp.float32)
    select_v[...] = jnp.zeros_like(select_v)
    for load in small_loads:
        load.wait()
    for m in range(batches):
        named = routes_v[0, m]
        weight = probs_v[0, m]
        example_row = examples_v[m].astype(jnp.float32)
        for place in range(2):
            expert = core if place == 0 else 1 - core
            hit = named == expert
            count_row = jnp.sum(jnp.where(hit, 1.0, 0.0), axis=0, keepdims=True)
            prob_row = jnp.sum(jnp.where(hit, weight, 0.0), axis=0, keepdims=True)
            count = jnp.sum(
                jnp.where(row_token == lane_token, count_row, 0.0), axis=1, keepdims=True
            )
            rank_row = jnp.sum(
                jnp.where(row_token < lane_token, count, 0.0), axis=0, keepdims=True
            )
            match = jnp.where(slot_row == rank_row, 1.0, 0.0) * count_row
            slot_prob = jnp.sum(match * prob_row, axis=1, keepdims=True)
            slot_example = jnp.sum(match * (example_row + 1.0), axis=1, keepdims=True) - 1.0
            first = place * rows + m * cap
            for at in (m * tokens, flat + m * tokens):
                select_v[first : first + cap, at : at + tokens] = match.astype(jnp.bfloat16)
            prob_v[first : first + cap, :] = jnp.broadcast_to(slot_prob, (cap, prob_v.shape[1]))
            wide = jnp.broadcast_to(slot_example.astype(jnp.int32), (cap, ex_out.shape[2]))
            if place == 0:
                ex_all[core, m] = wide
            else:
                ex_out[m] = wide
    ex_copy.start()

    @pl.when(high == last)
    def _():
        chain_in[...] = jnp.zeros_like(chain_in)

    own_load.wait()

    def feed(c):
        pair_copy(c).wait_send()

        @pl.when(c + IN_FLIGHT < chunks)
        def _():
            pair_copy(c + IN_FLIGHT).start()

    def carry(c):
        pair_copy(c).wait_recv()

        @pl.when(high < last)
        def _():
            chain_copy(c).wait_recv()

        own = own_v[:, :, pl.ds(pl.multiple_of(c * chunk, 128), chunk)].astype(jnp.float32)
        before = chain_in[c].astype(jnp.float32)

        @pl.when(high > 0)
        def _():
            total = before + own + pair_in[c].astype(jnp.float32)
            chain_out[c] = total.astype(jnp.bfloat16)
            chain_copy(c).start()

        swap_out[c] = (before + jnp.where(low == 1, own, 0.0)).astype(jnp.bfloat16)

    def rotate_hidden():
        hidden_load.wait()
        basis_load.wait()
        hid_own[...] = jnp.zeros_like(hid_own)

        def piece(p, _):
            acts = hidden_v[:, :, pl.ds(pl.multiple_of(p * piece_depth, 128), piece_depth)]
            hid_own[...] += jnp.dot(
                acts.reshape(batches * acts.shape[1], piece_depth),
                bh_v[pl.ds(pl.multiple_of(p * piece_depth, 128), piece_depth), :],
                preferred_element_type=jnp.float32,
            )
            return 0

        lax.fori_loop(0, pieces, piece, 0)
        hid_copy.start()

    def dispatch(c):
        swap_copy(c).wait_recv()
        select = select_v[...]
        slot_prob = prob_v[:, :1]

        def picked(cotangent):
            wide = cotangent.reshape(flat, chunk)
            coarse = wide.astype(jnp.bfloat16)
            fine = (wide - coarse.astype(jnp.float32)).astype(jnp.bfloat16)
            found = jnp.dot(
                select,
                jnp.concatenate([coarse, fine], axis=0),
                preferred_element_type=jnp.float32,
            )
            return (found * slot_prob).astype(jnp.bfloat16)

        def wide_top(half_index):
            return top_v[:, :, columns(half_index, c)].astype(jnp.float32)

        pair_term = jnp.where(low == 0, pair_in[c].astype(jnp.float32), 0.0)
        mine = picked(wide_top(low) + chain_in[c].astype(jnp.float32) + pair_term)
        rest = picked(wide_top(1 - low) + swap_in[c].astype(jnp.float32))
        rows_out[c, low] = mine[rows:]
        rows_out[c, 1 - low] = rest[rows:]
        rows_copy(c).start()
        rows_all[core, c, low] = mine[:rows]
        rows_all[core, c, 1 - low] = rest[:rows]

    def rotate_model(c):
        rows_copy(c).wait_recv()
        total = jnp.dot(
            jnp.concatenate(
                [
                    jnp.concatenate([rows_all[0, c, h], rows_all[1, c, h]], axis=0)
                    for h in range(2)
                ],
                axis=1,
            ),
            jnp.concatenate(
                [
                    bm_v[pl.ds(pl.multiple_of(h * half + c * chunk, 128), chunk), :]
                    for h in range(2)
                ],
                axis=0,
            ),
            preferred_element_type=jnp.float32,
        )

        @pl.when(c == 0)
        def _():
            model_sum[...] = total

        @pl.when(c > 0)
        def _():
            model_sum[...] += total

    def block_columns(index):
        return pl.ds(pl.multiple_of(index * cols, 128), cols)

    turns = cap // 2 + 1

    def padding(like):
        return [jnp.zeros((hid_t.shape[2] - group * 2 * turns * cap, like.shape[1]), jnp.float32)]

    def prepare_hidden():
        ex_copy.wait_recv()
        hid_copy.wait_recv()
        hid = (hid_own[...] + hid_in[...]).astype(jnp.bfloat16).astype(jnp.float32)
        for part in range(batches // group):
            blocks = []
            for m in range(part * group, (part + 1) * group):
                for owner in range(2):
                    first = m * 2 * cap + owner * cap
                    block = hid[first : first + cap]
                    ids = ex_all[owner, m].astype(jnp.float32)
                    for turn in range(turns):
                        share = 1.0 if turn in (0, cap // 2) else 2.0
                        if turn:
                            other = pltpu.roll(block, turn, 0)
                            other_ids = pltpu.roll(ids, turn, 0)
                        else:
                            other, other_ids = block, ids
                        same = jnp.where(ids == other_ids, share, 0.0)
                        blocks.append(block * other * same[:, :1])
            pairs = jnp.concatenate(blocks + padding(hid), axis=0)
            hid_t[part] = pairs.T.astype(jnp.bfloat16)

    def squares(part):
        blocks = []
        for m in range(part * group, (part + 1) * group):
            part_copy(m).wait_recv()
            for owner in range(2):
                first = owner * rows + m * cap
                block = model_sum[first : first + cap, block_columns(shard)]
                block = block + part_in[m, owner].astype(jnp.float32)
                block = block.astype(jnp.bfloat16).astype(jnp.float32)
                for turn in range(turns):
                    other = pltpu.roll(block, turn, 0) if turn else block
                    blocks.append(block * other)
        pairs = jnp.concatenate(blocks + padding(blocks[0]), axis=0).astype(jnp.bfloat16)
        return jnp.dot(hid_t[part], pairs, preferred_element_type=jnp.float32)

    early = high < last - 1
    held = jnp.minimum(chunks - 1, HOP_LAG * high)
    lag = held + SWAP_LAG
    model_lag = lag + ROWS_LAG

    @pl.when(early)
    def _():
        rotate_hidden()

    @pl.when(high < last)
    def _():
        lax.fori_loop(0, chunks, lambda c, _: (feed(c), 0)[1], 0)

    @pl.when(high == 0)
    def _():
        @pl.when(jnp.logical_not(early))
        def _():
            rotate_hidden()

        prepare_hidden()

    def step(k, _):
        @pl.when(k < chunks)
        def _():
            carry(k)

            @pl.when(high == last)
            def _():
                feed(k)

        @pl.when(jnp.logical_and(k == chunks - 1, jnp.logical_not(early)))
        def _():
            @pl.when(high > 0)
            def _():
                rotate_hidden()

        @pl.when(jnp.logical_and(k == chunks + 1, high > 0))
        def _():
            prepare_hidden()

        @pl.when(jnp.logical_and(k >= held, k < chunks + held))
        def _():
            swap_copy(k - held).start()

        @pl.when(k == lag)
        def _():
            top_load.wait()
            model_load.wait()

        @pl.when(jnp.logical_and(k >= lag, k < chunks + lag))
        def _():
            dispatch(k - lag)

        @pl.when(k >= model_lag)
        def _():
            rotate_model(k - model_lag)

        return 0

    lax.fori_loop(0, chunks + model_lag, step, 0)

    for m in range(batches):
        for owner in range(2):
            first = owner * rows + m * cap
            part_out[m, owner] = model_sum[
                first : first + cap, block_columns(1 - shard)
            ].astype(jnp.bfloat16)
        part_copy(m).start()
    out[0, 0] = squares(0)
    for part in range(1, batches // group):
        out[0, 0] += squares(part)

    for c in range(chunks):
        swap_copy(c).wait_send()
        rows_copy(c).wait_send()
    for m in range(batches):
        part_copy(m).wait_send()
    ex_copy.wait_send()
    hid_copy.wait_send()

    @pl.when(high > 0)
    def _():
        for c in range(chunks):
            chain_copy(c).wait_send()


def on_device(
    routes,
    route_probs,
    example_ids,
    top_cotangent,
    branch_cotangent,
    hidden_acts,
    basis_hidden,
    basis_model,
):
    sections = lax.axis_size("section")
    shards = lax.axis_size("shard")
    batches, tokens, width = top_cotangent.shape
    slots, depth = hidden_acts.shape[3:]
    cap = slots // lax.axis_size("expert")
    rank_hidden = basis_hidden.shape[3]
    cols = basis_model.shape[3] // shards
    half = width // 2
    chunk = CHUNK if half % CHUNK == 0 else 128
    chunks = half // chunk
    group = 2 if batches % 2 == 0 else 1
    pairs = -(-group * 2 * (cap // 2 + 1) * cap // 128) * 128
    bf16, f32 = jnp.bfloat16, jnp.float32
    vmem = pl.BlockSpec(memory_space=pltpu.VMEM)
    hbm = pl.BlockSpec(memory_space=pl.ANY)
    dma = pltpu.SemaphoreType.DMA
    moving = pltpu.VMEM((chunks, batches, tokens, chunk), bf16)
    routes = jnp.swapaxes(routes, 2, 3)
    route_probs = jnp.swapaxes(route_probs, 2, 3)
    flops = 2 * batches * slots * (depth * rank_hidden + width * cols * shards)
    square_sum = pl.pallas_call(
        functools.partial(kernel, sections),
        out_shape=jax.ShapeDtypeStruct((1, 1, rank_hidden, cols), f32),
        in_specs=[hbm] * 8,
        out_specs=vmem,
        scratch_shapes=[
            pltpu.VMEM(routes.shape, jnp.int32),
            pltpu.VMEM(route_probs.shape, f32),
            pltpu.VMEM(example_ids.shape, jnp.int32),
            pltpu.VMEM((batches, tokens, width), bf16),
            pltpu.VMEM((batches, tokens, half), bf16),
            pltpu.VMEM((batches, slots, depth), bf16),
            pltpu.VMEM((depth, rank_hidden), bf16),
            pltpu.VMEM((width, cols * shards), bf16),
            moving,
            moving,
            moving,
            moving,
            moving,
            pltpu.VMEM((2 * batches * cap, 2 * batches * tokens), bf16),
            pltpu.VMEM((2 * batches * cap, 128), f32),
            pltpu.VMEM((batches, cap, 128), jnp.int32),
            pltpu.VMEM((2, batches, cap, 128), jnp.int32),
            pltpu.VMEM((chunks, 2, batches * cap, chunk), bf16),
            pltpu.VMEM((2, chunks, 2, batches * cap, chunk), bf16),
            pltpu.VMEM((batches * slots, cols * shards), f32),
            pltpu.VMEM((batches, 2, cap, cols), bf16),
            pltpu.VMEM((batches, 2, cap, cols), bf16),
            pltpu.VMEM((batches * slots, rank_hidden), f32),
            pltpu.VMEM((batches * slots, rank_hidden), f32),
            pltpu.VMEM((batches // group, rank_hidden, pairs), bf16),
            dma((8,)),
        ]
        + [dma((chunks,))] * 8
        + [dma((batches,))] * 2
        + [dma((2,))] * 2,
        compiler_params=pltpu.CompilerParams(
            collective_id=0, has_side_effects=True, vmem_limit_bytes=60 * 1024 * 1024
        ),
        cost_estimate=pl.CostEstimate(
            flops=flops, bytes_accessed=16 * 1024 * 1024, transcendentals=0
        ),
    )(
        routes,
        route_probs,
        example_ids,
        top_cotangent,
        branch_cotangent,
        hidden_acts,
        basis_hidden,
        basis_model,
    )
    return square_sum / (batches * lax.axis_size("expert") * SEQS)


def solution(mesh):
    return jax.shard_map(
        on_device,
        mesh=mesh,
        in_specs=(
            P("section", None, "expert", None),
            P("section", None, "expert", None),
            P(None, "expert", None),
            P(None, "expert", "shard"),
            P("section", None, "expert", "shard"),
            P("section", "expert", None, None, "shard"),
            P("section", "expert", "shard", None),
            P("section", "expert", "shard", None),
        ),
        out_specs=P("section", "expert", None, "shard"),
        check_vma=False,
    )
```

```python
import functools

import jax
import jax.numpy as jnp
from jax import lax
from jax.experimental import pallas as pl
from jax.experimental.pallas import tpu as pltpu
from jax.sharding import PartitionSpec as P

SEQS = 2
CHUNK = 256
IN_FLIGHT = 3
SWAP_LAG = 2
ROWS_LAG = 2
HOP_LAG = 2
MESH = pl.DeviceIdType.MESH


def kernel(
    sections,
    routes,
    probs,
    examples,
    top,
    branch,
    hidden,
    basis_hidden,
    basis_model,
    out,
    routes_v,
    probs_v,
    examples_v,
    top_v,
    own_v,
    stage_v,
    hidden_v,
    bh_v,
    bm_v,
    pair_in,
    chain_in,
    chain_out,
    swap_out,
    swap_in,
    select_v,
    prob_v,
    ex_out,
    ex_all,
    rows_out,
    rows_all,
    model_sum,
    part_out,
    part_in,
    hid_own,
    hid_in,
    hid_t,
    local_sem,
    stage_sem,
    pair_s,
    pair_r,
    chain_s,
    chain_r,
    swap_s,
    swap_r,
    rows_s,
    rows_r,
    part_s,
    part_r,
    one_s,
    one_r,
):
    batches, tokens, width = top.shape
    half = width // 2
    chunks = pair_in.shape[0]
    chunk = pair_in.shape[3]
    cap = part_out.shape[2]
    rows = batches * cap
    flat = batches * tokens
    section = lax.axis_index("section")
    core = lax.axis_index("expert")
    shard = lax.axis_index("shard")
    low = lax.rem(section, 2)
    high = section // 2
    last = sections // 2 - 1
    partner = {"section": section + 1 - 2 * low}
    other_core = {"expert": 1 - core}
    other_shard = {"shard": 1 - shard}
    cols = part_out.shape[3]
    pieces = 4
    piece_depth = bh_v.shape[0] // pieces
    group = batches // hid_t.shape[0]

    def columns(half_index, index):
        return pl.ds(pl.multiple_of(half_index * half + index * chunk, 128), chunk)

    small_loads = [
        pltpu.make_async_copy(source, target, local_sem.at[index])
        for index, (source, target) in enumerate(
            ((routes, routes_v), (probs, probs_v), (examples, examples_v))
        )
    ]
    own_load = pltpu.make_async_copy(
        branch.at[0, :, :, pl.ds(pl.multiple_of(low * half, 128), half)], own_v, local_sem.at[3]
    )
    hidden_load = pltpu.make_async_copy(hidden.at[0, 0], hidden_v, local_sem.at[4])
    top_load = pltpu.make_async_copy(top, top_v, local_sem.at[5])
    model_load = pltpu.make_async_copy(basis_model.at[0, 0], bm_v, local_sem.at[6])
    basis_load = pltpu.make_async_copy(basis_hidden.at[0, 0], bh_v, local_sem.at[7])

    def stage_load(c):
        return pltpu.make_async_copy(
            branch.at[0, :, :, columns(1 - low, c)], stage_v.at[c], stage_sem.at[c]
        )

    for c in range(chunks):
        stage_load(c).start()
    for load in small_loads + [own_load]:
        load.start()

    barrier = pltpu.get_barrier_semaphore()
    for target in (partner, other_core, other_shard):
        pl.semaphore_signal(barrier, inc=1, device_id=target, device_id_type=MESH)

    @pl.when(high > 0)
    def _():
        pl.semaphore_signal(
            barrier, inc=1, device_id={"section": section - 2}, device_id_type=MESH
        )

    @pl.when(high < last)
    def _():
        pl.semaphore_signal(
            barrier, inc=1, device_id={"section": section + 2}, device_id_type=MESH
        )

    pl.semaphore_wait(
        barrier, 3 + jnp.where(high > 0, 1, 0) + jnp.where(high < last, 1, 0)
    )

    def remote(source, target, send, receive, device):
        return pltpu.make_async_remote_copy(
            src_ref=source,
            dst_ref=target,
            send_sem=send,
            recv_sem=receive,
            device_id=device,
            device_id_type=MESH,
        )

    def pair_copy(c):
        return remote(
            stage_v.at[c],
            pair_in.at[c],
            pair_s.at[c],
            pair_r.at[c],
            partner,
        )

    def chain_copy(c):
        return remote(
            chain_out.at[c], chain_in.at[c], chain_s.at[c], chain_r.at[c],
            {"section": section - 2},
        )

    def swap_copy(c):
        return remote(swap_out.at[c], swap_in.at[c], swap_s.at[c], swap_r.at[c], partner)

    def rows_copy(c):
        return remote(
            rows_out.at[c], rows_all.at[core, c], rows_s.at[c], rows_r.at[c], other_core
        )

    def part_copy(m):
        return remote(part_out.at[m], part_in.at[m], part_s.at[m], part_r.at[m], other_shard)

    ex_copy = remote(ex_out, ex_all.at[core], one_s.at[0], one_r.at[0], other_core)
    hid_copy = remote(hid_own, hid_in, one_s.at[1], one_r.at[1], other_shard)

    for c in range(min(IN_FLIGHT, chunks)):
        stage_load(c).wait()
        pair_copy(c).start()
    hidden_load.start()
    basis_load.start()
    top_load.start()
    model_load.start()

    lane_token = lax.broadcasted_iota(jnp.int32, (tokens, tokens), 1)
    row_token = lax.broadcasted_iota(jnp.int32, (tokens, tokens), 0)
    slot_row = lax.broadcasted_iota(jnp.int32, (cap, tokens), 0).astype(jnp.float32)
    select_v[...] = jnp.zeros_like(select_v)
    for load in small_loads:
        load.wait()
    for m in range(batches):
        named = routes_v[0, m]
        weight = probs_v[0, m]
        example_row = examples_v[m].astype(jnp.float32)
        for place in range(2):
            expert = core if place == 0 else 1 - core
            hit = named == expert
            count_row = jnp.sum(jnp.where(hit, 1.0, 0.0), axis=0, keepdims=True)
            prob_row = jnp.sum(jnp.where(hit, weight, 0.0), axis=0, keepdims=True)
            count = jnp.sum(
                jnp.where(row_token == lane_token, count_row, 0.0), axis=1, keepdims=True
            )
            rank_row = jnp.sum(
                jnp.where(row_token < lane_token, count, 0.0), axis=0, keepdims=True
            )
            match = jnp.where(slot_row == rank_row, 1.0, 0.0) * count_row
            slot_prob = jnp.sum(match * prob_row, axis=1, keepdims=True)
            slot_example = jnp.sum(match * (example_row + 1.0), axis=1, keepdims=True) - 1.0
            first = place * rows + m * cap
            for at in (m * tokens, flat + m * tokens):
                select_v[first : first + cap, at : at + tokens] = match.astype(jnp.bfloat16)
            prob_v[first : first + cap, :] = jnp.broadcast_to(slot_prob, (cap, prob_v.shape[1]))
            wide = jnp.broadcast_to(slot_example.astype(jnp.int32), (cap, ex_out.shape[2]))
            if place == 0:
                ex_all[core, m] = wide
            else:
                ex_out[m] = wide
    ex_copy.start()

    @pl.when(high == last)
    def _():
        chain_in[...] = jnp.zeros_like(chain_in)

    own_load.wait()

    def feed(c):
        @pl.when(c + IN_FLIGHT < chunks)
        def _():
            pair_copy(c).wait_send()
            stage_load(c + IN_FLIGHT).wait()
            pair_copy(c + IN_FLIGHT).start()

    def carry(c):
        pair_copy(c).wait_recv()

        @pl.when(high < last)
        def _():
            chain_copy(c).wait_recv()

        own = own_v[:, :, pl.ds(pl.multiple_of(c * chunk, 128), chunk)].astype(jnp.float32)
        before = chain_in[c].astype(jnp.float32)

        @pl.when(high > 0)
        def _():
            total = before + own + pair_in[c].astype(jnp.float32)
            chain_out[c] = total.astype(jnp.bfloat16)
            chain_copy(c).start()

        swap_out[c] = (before + jnp.where(low == 1, own, 0.0)).astype(jnp.bfloat16)

    def rotate_hidden():
        hidden_load.wait()
        basis_load.wait()
        hid_own[...] = jnp.zeros_like(hid_own)

        def piece(p, _):
            acts = hidden_v[:, :, pl.ds(pl.multiple_of(p * piece_depth, 128), piece_depth)]
            hid_own[...] += jnp.dot(
                acts.reshape(batches * acts.shape[1], piece_depth),
                bh_v[pl.ds(pl.multiple_of(p * piece_depth, 128), piece_depth), :],
                preferred_element_type=jnp.float32,
            )
            return 0

        lax.fori_loop(0, pieces, piece, 0)
        hid_copy.start()

    def dispatch(c):
        swap_copy(c).wait_recv()
        select = select_v[...]
        slot_prob = prob_v[:, :1]

        def picked(cotangent):
            wide = cotangent.reshape(flat, chunk)
            coarse = wide.astype(jnp.bfloat16)
            fine = (wide - coarse.astype(jnp.float32)).astype(jnp.bfloat16)
            found = jnp.dot(
                select,
                jnp.concatenate([coarse, fine], axis=0),
                preferred_element_type=jnp.float32,
            )
            return (found * slot_prob).astype(jnp.bfloat16)

        def wide_top(half_index):
            return top_v[:, :, columns(half_index, c)].astype(jnp.float32)

        pair_term = jnp.where(low == 0, pair_in[c].astype(jnp.float32), 0.0)
        mine = picked(wide_top(low) + chain_in[c].astype(jnp.float32) + pair_term)
        rest = picked(wide_top(1 - low) + swap_in[c].astype(jnp.float32))
        rows_out[c, low] = mine[rows:]
        rows_out[c, 1 - low] = rest[rows:]
        rows_copy(c).start()
        rows_all[core, c, low] = mine[:rows]
        rows_all[core, c, 1 - low] = rest[:rows]

    def rotate_model(c):
        rows_copy(c).wait_recv()
        total = jnp.dot(
            jnp.concatenate(
                [
                    jnp.concatenate([rows_all[0, c, h], rows_all[1, c, h]], axis=0)
                    for h in range(2)
                ],
                axis=1,
            ),
            jnp.concatenate(
                [
                    bm_v[pl.ds(pl.multiple_of(h * half + c * chunk, 128), chunk), :]
                    for h in range(2)
                ],
                axis=0,
            ),
            preferred_element_type=jnp.float32,
        )

        @pl.when(c == 0)
        def _():
            model_sum[...] = total

        @pl.when(c > 0)
        def _():
            model_sum[...] += total

    def block_columns(index):
        return pl.ds(pl.multiple_of(index * cols, 128), cols)

    turns = cap // 2 + 1

    def padding(like):
        return [jnp.zeros((hid_t.shape[2] - group * 2 * turns * cap, like.shape[1]), jnp.float32)]

    def prepare_hidden():
        ex_copy.wait_recv()
        hid_copy.wait_recv()
        hid = (hid_own[...] + hid_in[...]).astype(jnp.bfloat16).astype(jnp.float32)
        for part in range(batches // group):
            blocks = []
            for m in range(part * group, (part + 1) * group):
                for owner in range(2):
                    first = m * 2 * cap + owner * cap
                    block = hid[first : first + cap]
                    ids = ex_all[owner, m].astype(jnp.float32)
                    for turn in range(turns):
                        share = 1.0 if turn in (0, cap // 2) else 2.0
                        if turn:
                            other = pltpu.roll(block, turn, 0)
                            other_ids = pltpu.roll(ids, turn, 0)
                        else:
                            other, other_ids = block, ids
                        same = jnp.where(ids == other_ids, share, 0.0)
                        blocks.append(block * other * same[:, :1])
            pairs = jnp.concatenate(blocks + padding(hid), axis=0)
            hid_t[part] = pairs.T.astype(jnp.bfloat16)

    def squares(part):
        blocks = []
        for m in range(part * group, (part + 1) * group):
            part_copy(m).wait_recv()
            for owner in range(2):
                first = owner * rows + m * cap
                block = model_sum[first : first + cap, block_columns(shard)]
                block = block + part_in[m, owner].astype(jnp.float32)
                block = block.astype(jnp.bfloat16).astype(jnp.float32)
                for turn in range(turns):
                    other = pltpu.roll(block, turn, 0) if turn else block
                    blocks.append(block * other)
        pairs = jnp.concatenate(blocks + padding(blocks[0]), axis=0).astype(jnp.bfloat16)
        return jnp.dot(hid_t[part], pairs, preferred_element_type=jnp.float32)

    early = high < last - 1
    held = jnp.minimum(chunks - 1, HOP_LAG * high)
    lag = jnp.where(high > 0, jnp.maximum(chunks, held + SWAP_LAG), held + SWAP_LAG)
    model_lag = lag + ROWS_LAG

    @pl.when(early)
    def _():
        rotate_hidden()

    @pl.when(high < last)
    def _():
        lax.fori_loop(0, chunks, lambda c, _: (feed(c), 0)[1], 0)

    @pl.when(high == 0)
    def _():
        @pl.when(jnp.logical_not(early))
        def _():
            rotate_hidden()

    def step(k, _):
        @pl.when(k < chunks)
        def _():
            carry(k)

            @pl.when(high == last)
            def _():
                feed(k)

        @pl.when(jnp.logical_and(k >= held, k < chunks + held))
        def _():
            swap_copy(k - held).start()

        @pl.when(jnp.logical_and(k == chunks - 1, jnp.logical_not(early)))
        def _():
            @pl.when(high > 0)
            def _():
                rotate_hidden()

        @pl.when(k == jnp.where(high > 0, chunks + 1, chunks // 2))
        def _():
            prepare_hidden()

        @pl.when(k == lag)
        def _():
            top_load.wait()
            model_load.wait()

        @pl.when(jnp.logical_and(k >= lag, k < chunks + lag))
        def _():
            dispatch(k - lag)

        @pl.when(k >= model_lag)
        def _():
            rotate_model(k - model_lag)

        return 0

    lax.fori_loop(0, chunks + model_lag, step, 0)

    for m in range(batches):
        for owner in range(2):
            first = owner * rows + m * cap
            part_out[m, owner] = model_sum[
                first : first + cap, block_columns(1 - shard)
            ].astype(jnp.bfloat16)
        part_copy(m).start()
    out[0, 0] = squares(0)
    for part in range(1, batches // group):
        out[0, 0] += squares(part)

    for c in range(chunks):
        swap_copy(c).wait_send()
        rows_copy(c).wait_send()
    for c in range(max(chunks - IN_FLIGHT, 0), chunks):
        pair_copy(c).wait_send()
    for m in range(batches):
        part_copy(m).wait_send()
    ex_copy.wait_send()
    hid_copy.wait_send()

    @pl.when(high > 0)
    def _():
        for c in range(chunks):
            chain_copy(c).wait_send()


def on_device(
    routes,
    route_probs,
    example_ids,
    top_cotangent,
    branch_cotangent,
    hidden_acts,
    basis_hidden,
    basis_model,
):
    sections = lax.axis_size("section")
    shards = lax.axis_size("shard")
    batches, tokens, width = top_cotangent.shape
    slots, depth = hidden_acts.shape[3:]
    cap = slots // lax.axis_size("expert")
    rank_hidden = basis_hidden.shape[3]
    cols = basis_model.shape[3] // shards
    half = width // 2
    chunk = CHUNK if half % CHUNK == 0 else 128
    chunks = half // chunk
    group = 2 if batches % 2 == 0 else 1
    pairs = -(-group * 2 * (cap // 2 + 1) * cap // 128) * 128
    bf16, f32 = jnp.bfloat16, jnp.float32
    vmem = pl.BlockSpec(memory_space=pltpu.VMEM)
    hbm = pl.BlockSpec(memory_space=pl.ANY)
    dma = pltpu.SemaphoreType.DMA
    moving = pltpu.VMEM((chunks, batches, tokens, chunk), bf16)
    routes = jnp.swapaxes(routes, 2, 3)
    route_probs = jnp.swapaxes(route_probs, 2, 3)
    flops = 2 * batches * slots * (depth * rank_hidden + width * cols * shards)
    square_sum = pl.pallas_call(
        functools.partial(kernel, sections),
        out_shape=jax.ShapeDtypeStruct((1, 1, rank_hidden, cols), f32),
        in_specs=[hbm] * 8,
        out_specs=vmem,
        scratch_shapes=[
            pltpu.VMEM(routes.shape, jnp.int32),
            pltpu.VMEM(route_probs.shape, f32),
            pltpu.VMEM(example_ids.shape, jnp.int32),
            pltpu.VMEM((batches, tokens, width), bf16),
            pltpu.VMEM((batches, tokens, half), bf16),
            moving,
            pltpu.VMEM((batches, slots, depth), bf16),
            pltpu.VMEM((depth, rank_hidden), bf16),
            pltpu.VMEM((width, cols * shards), bf16),
            moving,
            moving,
            moving,
            moving,
            moving,
            pltpu.VMEM((2 * batches * cap, 2 * batches * tokens), bf16),
            pltpu.VMEM((2 * batches * cap, 128), f32),
            pltpu.VMEM((batches, cap, 128), jnp.int32),
            pltpu.VMEM((2, batches, cap, 128), jnp.int32),
            pltpu.VMEM((chunks, 2, batches * cap, chunk), bf16),
            pltpu.VMEM((2, chunks, 2, batches * cap, chunk), bf16),
            pltpu.VMEM((batches * slots, cols * shards), f32),
            pltpu.VMEM((batches, 2, cap, cols), bf16),
            pltpu.VMEM((batches, 2, cap, cols), bf16),
            pltpu.VMEM((batches * slots, rank_hidden), f32),
            pltpu.VMEM((batches * slots, rank_hidden), f32),
            pltpu.VMEM((batches // group, rank_hidden, pairs), bf16),
            dma((8,)),
        ]
        + [dma((chunks,))] * 9
        + [dma((batches,))] * 2
        + [dma((2,))] * 2,
        compiler_params=pltpu.CompilerParams(
            collective_id=0, has_side_effects=True, vmem_limit_bytes=60 * 1024 * 1024
        ),
        cost_estimate=pl.CostEstimate(
            flops=flops, bytes_accessed=16 * 1024 * 1024, transcendentals=0
        ),
    )(
        routes,
        route_probs,
        example_ids,
        top_cotangent,
        branch_cotangent,
        hidden_acts,
        basis_hidden,
        basis_model,
    )
    return square_sum / (batches * lax.axis_size("expert") * SEQS)


def solution(mesh):
    return jax.shard_map(
        on_device,
        mesh=mesh,
        in_specs=(
            P("section", None, "expert", None),
            P("section", None, "expert", None),
            P(None, "expert", None),
            P(None, "expert", "shard"),
            P("section", None, "expert", "shard"),
            P("section", "expert", None, None, "shard"),
            P("section", "expert", "shard", None),
            P("section", "expert", "shard", None),
        ),
        out_specs=P("section", "expert", None, "shard"),
        check_vma=False,
    )
```

```python
import functools

import jax
import jax.numpy as jnp
from jax import lax
from jax.experimental import pallas as pl
from jax.experimental.pallas import tpu as pltpu
from jax.sharding import PartitionSpec as P

SEQS = 2
CHUNK = 128
IN_FLIGHT = 4
SWAP_LAG = 3
ROWS_LAG = 2
HOP_LAG = 3
MESH = pl.DeviceIdType.MESH


def kernel(
    sections,
    routes,
    probs,
    examples,
    top,
    branch,
    hidden,
    basis_hidden,
    basis_model,
    out,
    routes_v,
    probs_v,
    examples_v,
    top_v,
    own_v,
    stage_v,
    hidden_v,
    bh_v,
    bm_v,
    pair_in,
    chain_in,
    chain_out,
    swap_out,
    swap_in,
    select_v,
    prob_v,
    ex_out,
    ex_all,
    rows_out,
    rows_all,
    model_sum,
    part_out,
    part_in,
    hid_own,
    hid_in,
    hid_t,
    local_sem,
    stage_sem,
    pair_s,
    pair_r,
    chain_s,
    chain_r,
    swap_s,
    swap_r,
    rows_s,
    rows_r,
    part_s,
    part_r,
    one_s,
    one_r,
):
    batches, tokens, width = top.shape
    half = width // 2
    chunks = pair_in.shape[0]
    chunk = pair_in.shape[3]
    cap = part_out.shape[2]
    rows = batches * cap
    flat = batches * tokens
    section = lax.axis_index("section")
    core = lax.axis_index("expert")
    shard = lax.axis_index("shard")
    low = lax.rem(section, 2)
    high = section // 2
    last = sections // 2 - 1
    partner = {"section": section + 1 - 2 * low}
    other_core = {"expert": 1 - core}
    other_shard = {"shard": 1 - shard}
    cols = part_out.shape[3]
    pieces = 4
    piece_depth = bh_v.shape[0] // pieces
    group = batches // hid_t.shape[0]

    def columns(half_index, index):
        return pl.ds(pl.multiple_of(half_index * half + index * chunk, 128), chunk)

    small_loads = [
        pltpu.make_async_copy(source, target, local_sem.at[index])
        for index, (source, target) in enumerate(
            ((routes, routes_v), (probs, probs_v), (examples, examples_v))
        )
    ]
    own_load = pltpu.make_async_copy(
        branch.at[0, :, :, pl.ds(pl.multiple_of(low * half, 128), half)], own_v, local_sem.at[3]
    )
    hidden_load = pltpu.make_async_copy(hidden.at[0, 0], hidden_v, local_sem.at[4])
    top_load = pltpu.make_async_copy(top, top_v, local_sem.at[5])
    model_load = pltpu.make_async_copy(basis_model.at[0, 0], bm_v, local_sem.at[6])
    basis_load = pltpu.make_async_copy(basis_hidden.at[0, 0], bh_v, local_sem.at[7])

    def stage_load(c):
        return pltpu.make_async_copy(
            branch.at[0, :, :, columns(1 - low, c)], stage_v.at[c], stage_sem.at[c]
        )

    for c in range(chunks):
        stage_load(c).start()
    for load in small_loads + [own_load]:
        load.start()

    barrier = pltpu.get_barrier_semaphore()
    for target in (partner, other_core, other_shard):
        pl.semaphore_signal(barrier, inc=1, device_id=target, device_id_type=MESH)

    @pl.when(high > 0)
    def _():
        pl.semaphore_signal(
            barrier, inc=1, device_id={"section": section - 2}, device_id_type=MESH
        )

    @pl.when(high < last)
    def _():
        pl.semaphore_signal(
            barrier, inc=1, device_id={"section": section + 2}, device_id_type=MESH
        )

    pl.semaphore_wait(
        barrier, 3 + jnp.where(high > 0, 1, 0) + jnp.where(high < last, 1, 0)
    )

    def remote(source, target, send, receive, device):
        return pltpu.make_async_remote_copy(
            src_ref=source,
            dst_ref=target,
            send_sem=send,
            recv_sem=receive,
            device_id=device,
            device_id_type=MESH,
        )

    def pair_copy(c):
        return remote(
            stage_v.at[c],
            pair_in.at[c],
            pair_s.at[c],
            pair_r.at[c],
            partner,
        )

    def chain_copy(c):
        return remote(
            chain_out.at[c], chain_in.at[c], chain_s.at[c], chain_r.at[c],
            {"section": section - 2},
        )

    def swap_copy(c):
        return remote(swap_out.at[c], swap_in.at[c], swap_s.at[c], swap_r.at[c], partner)

    def rows_copy(c):
        return remote(
            rows_out.at[c], rows_all.at[core, c], rows_s.at[c], rows_r.at[c], other_core
        )

    def part_copy(m):
        return remote(part_out.at[m], part_in.at[m], part_s.at[m], part_r.at[m], other_shard)

    ex_copy = remote(ex_out, ex_all.at[core], one_s.at[0], one_r.at[0], other_core)
    hid_copy = remote(hid_own, hid_in, one_s.at[1], one_r.at[1], other_shard)

    for c in range(min(IN_FLIGHT, chunks)):
        stage_load(c).wait()
        pair_copy(c).start()
    hidden_load.start()
    basis_load.start()
    top_load.start()
    model_load.start()

    def slot_tables():
        lane_token = lax.broadcasted_iota(jnp.int32, (tokens, tokens), 1)
        row_token = lax.broadcasted_iota(jnp.int32, (tokens, tokens), 0)
        slot_row = lax.broadcasted_iota(jnp.int32, (cap, tokens), 0).astype(jnp.float32)
        select_v[...] = jnp.zeros_like(select_v)
        for load in small_loads:
            load.wait()
        for m in range(batches):
            named = routes_v[0, m]
            weight = probs_v[0, m]
            example_row = examples_v[m].astype(jnp.float32)
            for place in range(2):
                expert = core if place == 0 else 1 - core
                hit = named == expert
                count_row = jnp.sum(jnp.where(hit, 1.0, 0.0), axis=0, keepdims=True)
                prob_row = jnp.sum(jnp.where(hit, weight, 0.0), axis=0, keepdims=True)
                count = jnp.sum(
                    jnp.where(row_token == lane_token, count_row, 0.0), axis=1, keepdims=True
                )
                rank_row = jnp.sum(
                    jnp.where(row_token < lane_token, count, 0.0), axis=0, keepdims=True
                )
                match = jnp.where(slot_row == rank_row, 1.0, 0.0) * count_row
                slot_prob = jnp.sum(match * prob_row, axis=1, keepdims=True)
                slot_example = jnp.sum(match * (example_row + 1.0), axis=1, keepdims=True) - 1.0
                first = place * rows + m * cap
                for at in (m * tokens, flat + m * tokens):
                    select_v[first : first + cap, at : at + tokens] = match.astype(jnp.bfloat16)
                prob_v[first : first + cap, :] = jnp.broadcast_to(slot_prob, (cap, prob_v.shape[1]))
                wide = jnp.broadcast_to(slot_example.astype(jnp.int32), (cap, ex_out.shape[2]))
                if place == 0:
                    ex_all[core, m] = wide
                else:
                    ex_out[m] = wide
        ex_copy.start()

    @pl.when(high < last)
    def _():
        slot_tables()

    @pl.when(high == last)
    def _():
        chain_in[...] = jnp.zeros_like(chain_in)

    own_load.wait()

    def feed(c):
        @pl.when(c + IN_FLIGHT < chunks)
        def _():
            pair_copy(c).wait_send()
            stage_load(c + IN_FLIGHT).wait()
            pair_copy(c + IN_FLIGHT).start()

    def carry(c):
        pair_copy(c).wait_recv()

        @pl.when(high < last)
        def _():
            chain_copy(c).wait_recv()

        own = own_v[:, :, pl.ds(pl.multiple_of(c * chunk, 128), chunk)].astype(jnp.float32)
        before = chain_in[c].astype(jnp.float32)

        @pl.when(high > 0)
        def _():
            total = before + own + pair_in[c].astype(jnp.float32)
            chain_out[c] = total.astype(jnp.bfloat16)
            chain_copy(c).start()

        swap_out[c] = (before + jnp.where(low == 1, own, 0.0)).astype(jnp.bfloat16)

    def rotate_hidden():
        hidden_load.wait()
        basis_load.wait()
        hid_own[...] = jnp.zeros_like(hid_own)

        def piece(p, _):
            acts = hidden_v[:, :, pl.ds(pl.multiple_of(p * piece_depth, 128), piece_depth)]
            hid_own[...] += jnp.dot(
                acts.reshape(batches * acts.shape[1], piece_depth),
                bh_v[pl.ds(pl.multiple_of(p * piece_depth, 128), piece_depth), :],
                preferred_element_type=jnp.float32,
            )
            return 0

        lax.fori_loop(0, pieces, piece, 0)
        hid_copy.start()

    def dispatch(c):
        swap_copy(c).wait_recv()
        select = select_v[...]
        slot_prob = prob_v[:, :1]

        def picked(cotangent):
            wide = cotangent.reshape(flat, chunk)
            coarse = wide.astype(jnp.bfloat16)
            fine = (wide - coarse.astype(jnp.float32)).astype(jnp.bfloat16)
            found = jnp.dot(
                select,
                jnp.concatenate([coarse, fine], axis=0),
                preferred_element_type=jnp.float32,
            )
            return (found * slot_prob).astype(jnp.bfloat16)

        def wide_top(half_index):
            return top_v[:, :, columns(half_index, c)].astype(jnp.float32)

        pair_term = jnp.where(low == 0, pair_in[c].astype(jnp.float32), 0.0)
        mine = picked(wide_top(low) + chain_in[c].astype(jnp.float32) + pair_term)
        rest = picked(wide_top(1 - low) + swap_in[c].astype(jnp.float32))
        rows_out[c, low] = mine[rows:]
        rows_out[c, 1 - low] = rest[rows:]
        rows_copy(c).start()
        rows_all[core, c, low] = mine[:rows]
        rows_all[core, c, 1 - low] = rest[:rows]

    def rotate_model(c):
        rows_copy(c).wait_recv()
        total = jnp.dot(
            jnp.concatenate(
                [
                    jnp.concatenate([rows_all[0, c, h], rows_all[1, c, h]], axis=0)
                    for h in range(2)
                ],
                axis=1,
            ),
            jnp.concatenate(
                [
                    bm_v[pl.ds(pl.multiple_of(h * half + c * chunk, 128), chunk), :]
                    for h in range(2)
                ],
                axis=0,
            ),
            preferred_element_type=jnp.float32,
        )

        @pl.when(c == 0)
        def _():
            model_sum[...] = total

        @pl.when(c > 0)
        def _():
            model_sum[...] += total

    def block_columns(index):
        return pl.ds(pl.multiple_of(index * cols, 128), cols)

    turns = cap // 2 + 1

    def padding(like):
        return [jnp.zeros((hid_t.shape[2] - group * 2 * turns * cap, like.shape[1]), jnp.float32)]

    def prepare_hidden():
        ex_copy.wait_recv()
        hid_copy.wait_recv()
        hid = (hid_own[...] + hid_in[...]).astype(jnp.bfloat16).astype(jnp.float32)
        for part in range(batches // group):
            blocks = []
            for m in range(part * group, (part + 1) * group):
                for owner in range(2):
                    first = m * 2 * cap + owner * cap
                    block = hid[first : first + cap]
                    ids = ex_all[owner, m].astype(jnp.float32)
                    for turn in range(turns):
                        share = 1.0 if turn in (0, cap // 2) else 2.0
                        if turn:
                            other = pltpu.roll(block, turn, 0)
                            other_ids = pltpu.roll(ids, turn, 0)
                        else:
                            other, other_ids = block, ids
                        same = jnp.where(ids == other_ids, share, 0.0)
                        blocks.append(block * other * same[:, :1])
            pairs = jnp.concatenate(blocks + padding(hid), axis=0)
            hid_t[part] = pairs.T.astype(jnp.bfloat16)

    def squares(part):
        blocks = []
        for m in range(part * group, (part + 1) * group):
            part_copy(m).wait_recv()
            for owner in range(2):
                first = owner * rows + m * cap
                block = model_sum[first : first + cap, block_columns(shard)]
                block = block + part_in[m, owner].astype(jnp.float32)
                block = block.astype(jnp.bfloat16).astype(jnp.float32)
                for turn in range(turns):
                    other = pltpu.roll(block, turn, 0) if turn else block
                    blocks.append(block * other)
        pairs = jnp.concatenate(blocks + padding(blocks[0]), axis=0).astype(jnp.bfloat16)
        return jnp.dot(hid_t[part], pairs, preferred_element_type=jnp.float32)

    early = high < last - 1
    held = jnp.minimum(chunks - 1, HOP_LAG * high)
    lag = jnp.where(high > 0, jnp.maximum(chunks, held + SWAP_LAG), held + SWAP_LAG)
    model_lag = lag + ROWS_LAG

    @pl.when(early)
    def _():
        rotate_hidden()

    @pl.when(high < last)
    def _():
        lax.fori_loop(0, chunks, lambda c, _: (feed(c), 0)[1], 0)

    @pl.when(high == 0)
    def _():
        @pl.when(jnp.logical_not(early))
        def _():
            rotate_hidden()

    def step(k, _):
        @pl.when(k < chunks)
        def _():
            carry(k)

            @pl.when(high == last)
            def _():
                feed(k)

        @pl.when(jnp.logical_and(k >= held, k < chunks + held))
        def _():
            swap_copy(k - held).start()

        @pl.when(jnp.logical_and(k == chunks - 1, high == last))
        def _():
            slot_tables()

        @pl.when(jnp.logical_and(k == chunks - 1, jnp.logical_not(early)))
        def _():
            @pl.when(high > 0)
            def _():
                rotate_hidden()

        @pl.when(k == jnp.where(high > 0, chunks + 1, chunks // 2))
        def _():
            prepare_hidden()

        @pl.when(k == lag)
        def _():
            top_load.wait()
            model_load.wait()

        @pl.when(jnp.logical_and(k >= lag, k < chunks + lag))
        def _():
            dispatch(k - lag)

        @pl.when(k >= model_lag)
        def _():
            rotate_model(k - model_lag)

        return 0

    lax.fori_loop(0, chunks + model_lag, step, 0)

    for m in range(batches):
        for owner in range(2):
            first = owner * rows + m * cap
            part_out[m, owner] = model_sum[
                first : first + cap, block_columns(1 - shard)
            ].astype(jnp.bfloat16)
        part_copy(m).start()
    out[0, 0] = squares(0)
    for part in range(1, batches // group):
        out[0, 0] += squares(part)

    for c in range(chunks):
        swap_copy(c).wait_send()
        rows_copy(c).wait_send()
    for c in range(max(chunks - IN_FLIGHT, 0), chunks):
        pair_copy(c).wait_send()
    for m in range(batches):
        part_copy(m).wait_send()
    ex_copy.wait_send()
    hid_copy.wait_send()

    @pl.when(high > 0)
    def _():
        for c in range(chunks):
            chain_copy(c).wait_send()


def on_device(
    routes,
    route_probs,
    example_ids,
    top_cotangent,
    branch_cotangent,
    hidden_acts,
    basis_hidden,
    basis_model,
):
    sections = lax.axis_size("section")
    shards = lax.axis_size("shard")
    batches, tokens, width = top_cotangent.shape
    slots, depth = hidden_acts.shape[3:]
    cap = slots // lax.axis_size("expert")
    rank_hidden = basis_hidden.shape[3]
    cols = basis_model.shape[3] // shards
    half = width // 2
    chunk = CHUNK if half % CHUNK == 0 else 128
    chunks = half // chunk
    group = 2 if batches % 2 == 0 else 1
    pairs = -(-group * 2 * (cap // 2 + 1) * cap // 128) * 128
    bf16, f32 = jnp.bfloat16, jnp.float32
    vmem = pl.BlockSpec(memory_space=pltpu.VMEM)
    hbm = pl.BlockSpec(memory_space=pl.ANY)
    dma = pltpu.SemaphoreType.DMA
    moving = pltpu.VMEM((chunks, batches, tokens, chunk), bf16)
    routes = jnp.swapaxes(routes, 2, 3)
    route_probs = jnp.swapaxes(route_probs, 2, 3)
    flops = 2 * batches * slots * (depth * rank_hidden + width * cols * shards)
    square_sum = pl.pallas_call(
        functools.partial(kernel, sections),
        out_shape=jax.ShapeDtypeStruct((1, 1, rank_hidden, cols), f32),
        in_specs=[hbm] * 8,
        out_specs=vmem,
        scratch_shapes=[
            pltpu.VMEM(routes.shape, jnp.int32),
            pltpu.VMEM(route_probs.shape, f32),
            pltpu.VMEM(example_ids.shape, jnp.int32),
            pltpu.VMEM((batches, tokens, width), bf16),
            pltpu.VMEM((batches, tokens, half), bf16),
            moving,
            pltpu.VMEM((batches, slots, depth), bf16),
            pltpu.VMEM((depth, rank_hidden), bf16),
            pltpu.VMEM((width, cols * shards), bf16),
            moving,
            moving,
            moving,
            moving,
            moving,
            pltpu.VMEM((2 * batches * cap, 2 * batches * tokens), bf16),
            pltpu.VMEM((2 * batches * cap, 128), f32),
            pltpu.VMEM((batches, cap, 128), jnp.int32),
            pltpu.VMEM((2, batches, cap, 128), jnp.int32),
            pltpu.VMEM((chunks, 2, batches * cap, chunk), bf16),
            pltpu.VMEM((2, chunks, 2, batches * cap, chunk), bf16),
            pltpu.VMEM((batches * slots, cols * shards), f32),
            pltpu.VMEM((batches, 2, cap, cols), bf16),
            pltpu.VMEM((batches, 2, cap, cols), bf16),
            pltpu.VMEM((batches * slots, rank_hidden), f32),
            pltpu.VMEM((batches * slots, rank_hidden), f32),
            pltpu.VMEM((batches // group, rank_hidden, pairs), bf16),
            dma((8,)),
        ]
        + [dma((chunks,))] * 9
        + [dma((batches,))] * 2
        + [dma((2,))] * 2,
        compiler_params=pltpu.CompilerParams(
            collective_id=0, has_side_effects=True, vmem_limit_bytes=60 * 1024 * 1024
        ),
        cost_estimate=pl.CostEstimate(
            flops=flops, bytes_accessed=16 * 1024 * 1024, transcendentals=0
        ),
    )(
        routes,
        route_probs,
        example_ids,
        top_cotangent,
        branch_cotangent,
        hidden_acts,
        basis_hidden,
        basis_model,
    )
    return square_sum / (batches * lax.axis_size("expert") * SEQS)


def solution(mesh):
    return jax.shard_map(
        on_device,
        mesh=mesh,
        in_specs=(
            P("section", None, "expert", None),
            P("section", None, "expert", None),
            P(None, "expert", None),
            P(None, "expert", "shard"),
            P("section", None, "expert", "shard"),
            P("section", "expert", None, None, "shard"),
            P("section", "expert", "shard", None),
            P("section", "expert", "shard", None),
        ),
        out_specs=P("section", "expert", None, "shard"),
        check_vma=False,
    )
```

```python
import functools

import jax
import jax.numpy as jnp
from jax import lax
from jax.experimental import pallas as pl
from jax.experimental.pallas import tpu as pltpu
from jax.sharding import PartitionSpec as P

SEQS = 2
CHUNK = 256
IN_FLIGHT = 3
SWAP_LAG = 2
ROWS_LAG = 2
HOP_LAG = 2
MESH = pl.DeviceIdType.MESH


def kernel(
    sections,
    routes,
    probs,
    examples,
    top,
    branch,
    hidden,
    basis_hidden,
    basis_model,
    out,
    routes_v,
    probs_v,
    examples_v,
    top_v,
    own_v,
    stage_v,
    hidden_v,
    bh_v,
    bm_v,
    pair_in,
    chain_in,
    chain_out,
    swap_out,
    swap_in,
    select_v,
    prob_v,
    ex_out,
    ex_all,
    rows_out,
    rows_all,
    model_sum,
    part_out,
    part_in,
    hid_own,
    hid_in,
    hid_t,
    local_sem,
    stage_sem,
    pair_s,
    pair_r,
    chain_s,
    chain_r,
    swap_s,
    swap_r,
    rows_s,
    rows_r,
    part_s,
    part_r,
    one_s,
    one_r,
):
    batches, tokens, width = top.shape
    half = width // 2
    chunks = pair_in.shape[0]
    chunk = pair_in.shape[3]
    cap = part_out.shape[2]
    rows = batches * cap
    flat = batches * tokens
    section = lax.axis_index("section")
    core = lax.axis_index("expert")
    shard = lax.axis_index("shard")
    low = lax.rem(section, 2)
    high = section // 2
    last = sections // 2 - 1
    partner = {"section": section + 1 - 2 * low}
    other_core = {"expert": 1 - core}
    other_shard = {"shard": 1 - shard}
    cols = part_out.shape[3]
    pieces = 4
    piece_depth = bh_v.shape[0] // pieces
    group = batches // hid_t.shape[0]

    def columns(half_index, index):
        return pl.ds(pl.multiple_of(half_index * half + index * chunk, 128), chunk)

    small_loads = [
        pltpu.make_async_copy(source, target, local_sem.at[index])
        for index, (source, target) in enumerate(
            ((routes, routes_v), (probs, probs_v), (examples, examples_v))
        )
    ]
    own_load = pltpu.make_async_copy(
        branch.at[0, :, :, pl.ds(pl.multiple_of(low * half, 128), half)], own_v, local_sem.at[3]
    )
    hidden_load = pltpu.make_async_copy(hidden.at[0, 0], hidden_v, local_sem.at[4])
    top_load = pltpu.make_async_copy(top, top_v, local_sem.at[5])
    model_load = pltpu.make_async_copy(basis_model.at[0, 0], bm_v, local_sem.at[6])
    basis_load = pltpu.make_async_copy(basis_hidden.at[0, 0], bh_v, local_sem.at[7])

    def stage_load(c):
        return pltpu.make_async_copy(
            branch.at[0, :, :, columns(1 - low, c)], stage_v.at[c], stage_sem.at[c]
        )

    for c in range(chunks):
        stage_load(c).start()
    for load in small_loads + [own_load]:
        load.start()

    barrier = pltpu.get_barrier_semaphore()
    for target in (partner, other_core, other_shard):
        pl.semaphore_signal(barrier, inc=1, device_id=target, device_id_type=MESH)

    @pl.when(high > 0)
    def _():
        pl.semaphore_signal(
            barrier, inc=1, device_id={"section": section - 2}, device_id_type=MESH
        )

    @pl.when(high < last)
    def _():
        pl.semaphore_signal(
            barrier, inc=1, device_id={"section": section + 2}, device_id_type=MESH
        )

    pl.semaphore_wait(
        barrier, 3 + jnp.where(high > 0, 1, 0) + jnp.where(high < last, 1, 0)
    )

    def remote(source, target, send, receive, device):
        return pltpu.make_async_remote_copy(
            src_ref=source,
            dst_ref=target,
            send_sem=send,
            recv_sem=receive,
            device_id=device,
            device_id_type=MESH,
        )

    def pair_copy(c):
        return remote(
            stage_v.at[c],
            pair_in.at[c],
            pair_s.at[c],
            pair_r.at[c],
            partner,
        )

    def chain_copy(c):
        return remote(
            chain_out.at[c], chain_in.at[c], chain_s.at[c], chain_r.at[c],
            {"section": section - 2},
        )

    def swap_copy(c):
        return remote(swap_out.at[c], swap_in.at[c], swap_s.at[c], swap_r.at[c], partner)

    def rows_copy(c):
        return remote(
            rows_out.at[c], rows_all.at[core, c], rows_s.at[c], rows_r.at[c], other_core
        )

    def part_copy(m):
        return remote(part_out.at[m], part_in.at[m], part_s.at[m], part_r.at[m], other_shard)

    ex_copy = remote(ex_out, ex_all.at[core], one_s.at[0], one_r.at[0], other_core)
    hid_copy = remote(hid_own, hid_in, one_s.at[1], one_r.at[1], other_shard)

    for c in range(min(IN_FLIGHT, chunks)):
        stage_load(c).wait()
        pair_copy(c).start()
    hidden_load.start()
    basis_load.start()
    top_load.start()
    model_load.start()

    def slot_tables():
        lane_token = lax.broadcasted_iota(jnp.int32, (tokens, tokens), 1)
        row_token = lax.broadcasted_iota(jnp.int32, (tokens, tokens), 0)
        slot_row = lax.broadcasted_iota(jnp.int32, (cap, tokens), 0).astype(jnp.float32)
        select_v[...] = jnp.zeros_like(select_v)
        for load in small_loads:
            load.wait()
        for m in range(batches):
            named = routes_v[0, m]
            weight = probs_v[0, m]
            example_row = examples_v[m].astype(jnp.float32)
            for place in range(2):
                expert = core if place == 0 else 1 - core
                hit = named == expert
                count_row = jnp.sum(jnp.where(hit, 1.0, 0.0), axis=0, keepdims=True)
                prob_row = jnp.sum(jnp.where(hit, weight, 0.0), axis=0, keepdims=True)
                count = jnp.sum(
                    jnp.where(row_token == lane_token, count_row, 0.0), axis=1, keepdims=True
                )
                rank_row = jnp.sum(
                    jnp.where(row_token < lane_token, count, 0.0), axis=0, keepdims=True
                )
                match = jnp.where(slot_row == rank_row, 1.0, 0.0) * count_row
                slot_prob = jnp.sum(match * prob_row, axis=1, keepdims=True)
                slot_example = jnp.sum(match * (example_row + 1.0), axis=1, keepdims=True) - 1.0
                first = place * rows + m * cap
                for at in (m * tokens, flat + m * tokens):
                    select_v[first : first + cap, at : at + tokens] = match.astype(jnp.bfloat16)
                prob_v[first : first + cap, :] = jnp.broadcast_to(slot_prob, (cap, prob_v.shape[1]))
                wide = jnp.broadcast_to(slot_example.astype(jnp.int32), (cap, ex_out.shape[2]))
                if place == 0:
                    ex_all[core, m] = wide
                else:
                    ex_out[m] = wide
        ex_copy.start()

    @pl.when(high < last)
    def _():
        slot_tables()

    @pl.when(high == last)
    def _():
        chain_in[...] = jnp.zeros_like(chain_in)

    own_load.wait()

    def feed(c):
        @pl.when(c + IN_FLIGHT < chunks)
        def _():
            pair_copy(c).wait_send()
            stage_load(c + IN_FLIGHT).wait()
            pair_copy(c + IN_FLIGHT).start()

    def carry(c):
        pair_copy(c).wait_recv()

        @pl.when(high < last)
        def _():
            chain_copy(c).wait_recv()

        own = own_v[:, :, pl.ds(pl.multiple_of(c * chunk, 128), chunk)].astype(jnp.float32)
        before = chain_in[c].astype(jnp.float32)

        @pl.when(high > 0)
        def _():
            total = before + own + pair_in[c].astype(jnp.float32)
            chain_out[c] = total.astype(jnp.bfloat16)
            chain_copy(c).start()

        swap_out[c] = (before + jnp.where(low == 1, own, 0.0)).astype(jnp.bfloat16)

    def rotate_hidden():
        hidden_load.wait()
        basis_load.wait()
        hid_own[...] = jnp.zeros_like(hid_own)

        def piece(p, _):
            acts = hidden_v[:, :, pl.ds(pl.multiple_of(p * piece_depth, 128), piece_depth)]
            hid_own[...] += jnp.dot(
                acts.reshape(batches * acts.shape[1], piece_depth),
                bh_v[pl.ds(pl.multiple_of(p * piece_depth, 128), piece_depth), :],
                preferred_element_type=jnp.float32,
            )
            return 0

        lax.fori_loop(0, pieces, piece, 0)
        hid_copy.start()

    def dispatch(c):
        swap_copy(c).wait_recv()
        select = select_v[...]
        slot_prob = jnp.concatenate([prob_v[...]] * (chunk // prob_v.shape[1]), axis=1)

        def picked(cotangent):
            wide = cotangent.reshape(flat, chunk)
            coarse = wide.astype(jnp.bfloat16)
            fine = (wide - coarse.astype(jnp.float32)).astype(jnp.bfloat16)
            found = jnp.dot(
                select,
                jnp.concatenate([coarse, fine], axis=0),
                preferred_element_type=jnp.float32,
            )
            return (found * slot_prob).astype(jnp.bfloat16)

        def wide_top(half_index):
            return top_v[:, :, columns(half_index, c)].astype(jnp.float32)

        pair_term = jnp.where(low == 0, pair_in[c].astype(jnp.float32), 0.0)
        mine = picked(wide_top(low) + chain_in[c].astype(jnp.float32) + pair_term)
        rest = picked(wide_top(1 - low) + swap_in[c].astype(jnp.float32))
        rows_out[c, low] = mine[rows:]
        rows_out[c, 1 - low] = rest[rows:]
        rows_copy(c).start()
        rows_all[core, c, low] = mine[:rows]
        rows_all[core, c, 1 - low] = rest[:rows]

    batch = 2 if chunks % 2 == 0 else 1

    def rotate_model(index):
        each = [(index * batch + part, h) for part in range(batch) for h in range(2)]
        for part in range(batch):
            rows_copy(index * batch + part).wait_recv()
        total = jnp.dot(
            jnp.concatenate(
                [
                    jnp.concatenate([rows_all[0, c, h], rows_all[1, c, h]], axis=0)
                    for c, h in each
                ],
                axis=1,
            ),
            jnp.concatenate(
                [
                    bm_v[pl.ds(pl.multiple_of(h * half + c * chunk, 128), chunk), :]
                    for c, h in each
                ],
                axis=0,
            ),
            preferred_element_type=jnp.float32,
        )

        @pl.when(index == 0)
        def _():
            model_sum[...] = total

        @pl.when(index > 0)
        def _():
            model_sum[...] += total

    def block_columns(index):
        return pl.ds(pl.multiple_of(index * cols, 128), cols)

    turns = cap // 2 + 1

    def padding(like):
        return [jnp.zeros((hid_t.shape[2] - group * 2 * turns * cap, like.shape[1]), jnp.float32)]

    def prepare_hidden():
        ex_copy.wait_recv()
        hid_copy.wait_recv()
        hid = (hid_own[...] + hid_in[...]).astype(jnp.bfloat16).astype(jnp.float32)
        for part in range(batches // group):
            blocks = []
            for m in range(part * group, (part + 1) * group):
                for owner in range(2):
                    first = m * 2 * cap + owner * cap
                    block = hid[first : first + cap]
                    ids = ex_all[owner, m].astype(jnp.float32)
                    for turn in range(turns):
                        share = 1.0 if turn in (0, cap // 2) else 2.0
                        if turn:
                            other = pltpu.roll(block, turn, 0)
                            other_ids = pltpu.roll(ids, turn, 0)
                        else:
                            other, other_ids = block, ids
                        same = jnp.where(ids == other_ids, share, 0.0)
                        blocks.append(block * other * same[:, :1])
            pairs = jnp.concatenate(blocks + padding(hid), axis=0)
            hid_t[part] = pairs.T.astype(jnp.bfloat16)

    def squares(part):
        blocks = []
        for m in range(part * group, (part + 1) * group):
            part_copy(m).wait_recv()
            for owner in range(2):
                first = owner * rows + m * cap
                block = model_sum[first : first + cap, block_columns(shard)]
                block = block + part_in[m, owner].astype(jnp.float32)
                block = block.astype(jnp.bfloat16).astype(jnp.float32)
                for turn in range(turns):
                    other = pltpu.roll(block, turn, 0) if turn else block
                    blocks.append(block * other)
        pairs = jnp.concatenate(blocks + padding(blocks[0]), axis=0).astype(jnp.bfloat16)
        return jnp.dot(hid_t[part], pairs, preferred_element_type=jnp.float32)

    early = high < last - 1
    held = jnp.minimum(chunks - 1, HOP_LAG * high)
    lag = jnp.where(high > 0, jnp.maximum(chunks, held + SWAP_LAG), held + SWAP_LAG)
    model_lag = lag + ROWS_LAG - 1

    @pl.when(early)
    def _():
        rotate_hidden()

    @pl.when(high < last)
    def _():
        lax.fori_loop(0, chunks, lambda c, _: (feed(c), 0)[1], 0)

    @pl.when(high == 0)
    def _():
        @pl.when(jnp.logical_not(early))
        def _():
            rotate_hidden()

    def step(k, _):
        @pl.when(k < chunks)
        def _():
            carry(k)

            @pl.when(high == last)
            def _():
                feed(k)

        @pl.when(jnp.logical_and(k >= held, k < chunks + held))
        def _():
            swap_copy(k - held).start()

        @pl.when(jnp.logical_and(k == chunks - 1, high == last))
        def _():
            slot_tables()

        @pl.when(jnp.logical_and(k == chunks - 1, jnp.logical_not(early)))
        def _():
            @pl.when(high > 0)
            def _():
                rotate_hidden()

        @pl.when(k == jnp.where(high > 0, chunks + 1, chunks // 2))
        def _():
            prepare_hidden()

        @pl.when(k == lag)
        def _():
            top_load.wait()
            model_load.wait()

        @pl.when(jnp.logical_and(k >= lag, k < chunks + lag))
        def _():
            dispatch(k - lag)

        ready = k - model_lag

        @pl.when(jnp.logical_and(ready >= 0, lax.rem(ready + batch, batch) == batch - 1))
        def _():
            rotate_model(ready // batch)

        return 0

    lax.fori_loop(0, chunks + model_lag, step, 0)

    for m in range(batches):
        for owner in range(2):
            first = owner * rows + m * cap
            part_out[m, owner] = model_sum[
                first : first + cap, block_columns(1 - shard)
            ].astype(jnp.bfloat16)
        part_copy(m).start()
    out[0, 0] = squares(0)
    for part in range(1, batches // group):
        out[0, 0] += squares(part)

    for c in range(chunks):
        swap_copy(c).wait_send()
        rows_copy(c).wait_send()
    for c in range(max(chunks - IN_FLIGHT, 0), chunks):
        pair_copy(c).wait_send()
    for m in range(batches):
        part_copy(m).wait_send()
    ex_copy.wait_send()
    hid_copy.wait_send()

    @pl.when(high > 0)
    def _():
        for c in range(chunks):
            chain_copy(c).wait_send()


def on_device(
    routes,
    route_probs,
    example_ids,
    top_cotangent,
    branch_cotangent,
    hidden_acts,
    basis_hidden,
    basis_model,
):
    sections = lax.axis_size("section")
    shards = lax.axis_size("shard")
    batches, tokens, width = top_cotangent.shape
    slots, depth = hidden_acts.shape[3:]
    cap = slots // lax.axis_size("expert")
    rank_hidden = basis_hidden.shape[3]
    cols = basis_model.shape[3] // shards
    half = width // 2
    chunk = CHUNK if half % CHUNK == 0 else 128
    chunks = half // chunk
    group = 2 if batches % 2 == 0 else 1
    pairs = -(-group * 2 * (cap // 2 + 1) * cap // 128) * 128
    bf16, f32 = jnp.bfloat16, jnp.float32
    vmem = pl.BlockSpec(memory_space=pltpu.VMEM)
    hbm = pl.BlockSpec(memory_space=pl.ANY)
    dma = pltpu.SemaphoreType.DMA
    moving = pltpu.VMEM((chunks, batches, tokens, chunk), bf16)
    routes = jnp.swapaxes(routes, 2, 3)
    route_probs = jnp.swapaxes(route_probs, 2, 3)
    flops = 2 * batches * slots * (depth * rank_hidden + width * cols * shards)
    square_sum = pl.pallas_call(
        functools.partial(kernel, sections),
        out_shape=jax.ShapeDtypeStruct((1, 1, rank_hidden, cols), f32),
        in_specs=[hbm] * 8,
        out_specs=vmem,
        scratch_shapes=[
            pltpu.VMEM(routes.shape, jnp.int32),
            pltpu.VMEM(route_probs.shape, f32),
            pltpu.VMEM(example_ids.shape, jnp.int32),
            pltpu.VMEM((batches, tokens, width), bf16),
            pltpu.VMEM((batches, tokens, half), bf16),
            moving,
            pltpu.VMEM((batches, slots, depth), bf16),
            pltpu.VMEM((depth, rank_hidden), bf16),
            pltpu.VMEM((width, cols * shards), bf16),
            moving,
            moving,
            moving,
            moving,
            moving,
            pltpu.VMEM((2 * batches * cap, 2 * batches * tokens), bf16),
            pltpu.VMEM((2 * batches * cap, 128), f32),
            pltpu.VMEM((batches, cap, 128), jnp.int32),
            pltpu.VMEM((2, batches, cap, 128), jnp.int32),
            pltpu.VMEM((chunks, 2, batches * cap, chunk), bf16),
            pltpu.VMEM((2, chunks, 2, batches * cap, chunk), bf16),
            pltpu.VMEM((batches * slots, cols * shards), f32),
            pltpu.VMEM((batches, 2, cap, cols), bf16),
            pltpu.VMEM((batches, 2, cap, cols), bf16),
            pltpu.VMEM((batches * slots, rank_hidden), f32),
            pltpu.VMEM((batches * slots, rank_hidden), f32),
            pltpu.VMEM((batches // group, rank_hidden, pairs), bf16),
            dma((8,)),
        ]
        + [dma((chunks,))] * 9
        + [dma((batches,))] * 2
        + [dma((2,))] * 2,
        compiler_params=pltpu.CompilerParams(
            collective_id=0, has_side_effects=True, vmem_limit_bytes=60 * 1024 * 1024
        ),
        cost_estimate=pl.CostEstimate(
            flops=flops, bytes_accessed=16 * 1024 * 1024, transcendentals=0
        ),
    )(
        routes,
        route_probs,
        example_ids,
        top_cotangent,
        branch_cotangent,
        hidden_acts,
        basis_hidden,
        basis_model,
    )
    return square_sum / (batches * lax.axis_size("expert") * SEQS)


def solution(mesh):
    return jax.shard_map(
        on_device,
        mesh=mesh,
        in_specs=(
            P("section", None, "expert", None),
            P("section", None, "expert", None),
            P(None, "expert", None),
            P(None, "expert", "shard"),
            P("section", None, "expert", "shard"),
            P("section", "expert", None, None, "shard"),
            P("section", "expert", "shard", None),
            P("section", "expert", "shard", None),
        ),
        out_specs=P("section", "expert", None, "shard"),
        check_vma=False,
    )
```

```python
import functools

import jax
import jax.numpy as jnp
from jax import lax
from jax.experimental import pallas as pl
from jax.experimental.pallas import tpu as pltpu
from jax.sharding import PartitionSpec as P

SEQS = 2
CHUNK = 256
IN_FLIGHT = 3
SWAP_LAG = 2
ROWS_LAG = 2
HOP_LAG = 2
MESH = pl.DeviceIdType.MESH


def kernel(
    sections,
    routes,
    probs,
    examples,
    top,
    branch,
    hidden,
    basis_hidden,
    basis_model,
    out,
    routes_v,
    probs_v,
    examples_v,
    top_v,
    own_v,
    stage_v,
    hidden_v,
    bh_v,
    bm_v,
    pair_in,
    chain_in,
    chain_out,
    swap_out,
    swap_in,
    select_v,
    prob_v,
    ex_out,
    ex_all,
    rows_out,
    rows_all,
    model_sum,
    part_out,
    part_in,
    hid_own,
    hid_in,
    hid_t,
    local_sem,
    stage_sem,
    pair_s,
    pair_r,
    chain_s,
    chain_r,
    swap_s,
    swap_r,
    rows_s,
    rows_r,
    part_s,
    part_r,
    one_s,
    one_r,
):
    batches, tokens, width = top.shape
    half = width // 2
    chunks = pair_in.shape[0]
    chunk = pair_in.shape[3]
    cap = part_out.shape[2]
    rows = batches * cap
    flat = batches * tokens
    section = lax.axis_index("section")
    core = lax.axis_index("expert")
    shard = lax.axis_index("shard")
    low = lax.rem(section, 2)
    high = section // 2
    last = sections // 2 - 1
    partner = {"section": section + 1 - 2 * low}
    other_core = {"expert": 1 - core}
    other_shard = {"shard": 1 - shard}
    cols = part_out.shape[3]
    pieces = 4
    piece_depth = bh_v.shape[0] // pieces
    group = batches // hid_t.shape[0]

    def columns(half_index, index):
        return pl.ds(pl.multiple_of(half_index * half + index * chunk, 128), chunk)

    small_loads = [
        pltpu.make_async_copy(source, target, local_sem.at[index])
        for index, (source, target) in enumerate(
            ((routes, routes_v), (probs, probs_v), (examples, examples_v))
        )
    ]
    own_load = pltpu.make_async_copy(
        branch.at[0, :, :, pl.ds(pl.multiple_of(low * half, 128), half)], own_v, local_sem.at[3]
    )
    hidden_load = pltpu.make_async_copy(hidden.at[0, 0], hidden_v, local_sem.at[4])
    top_load = pltpu.make_async_copy(top, top_v, local_sem.at[5])
    model_load = pltpu.make_async_copy(basis_model.at[0, 0], bm_v, local_sem.at[6])
    basis_load = pltpu.make_async_copy(basis_hidden.at[0, 0], bh_v, local_sem.at[7])

    def stage_load(c):
        return pltpu.make_async_copy(
            branch.at[0, :, :, columns(1 - low, c)], stage_v.at[c], stage_sem.at[c]
        )

    for c in range(chunks):
        stage_load(c).start()
    for load in small_loads + [own_load]:
        load.start()

    barrier = pltpu.get_barrier_semaphore()
    for target in (partner, other_core, other_shard):
        pl.semaphore_signal(barrier, inc=1, device_id=target, device_id_type=MESH)

    @pl.when(high > 0)
    def _():
        pl.semaphore_signal(
            barrier, inc=1, device_id={"section": section - 2}, device_id_type=MESH
        )

    @pl.when(high < last)
    def _():
        pl.semaphore_signal(
            barrier, inc=1, device_id={"section": section + 2}, device_id_type=MESH
        )

    pl.semaphore_wait(
        barrier, 3 + jnp.where(high > 0, 1, 0) + jnp.where(high < last, 1, 0)
    )

    def remote(source, target, send, receive, device):
        return pltpu.make_async_remote_copy(
            src_ref=source,
            dst_ref=target,
            send_sem=send,
            recv_sem=receive,
            device_id=device,
            device_id_type=MESH,
        )

    def pair_copy(c):
        return remote(
            stage_v.at[c],
            pair_in.at[c],
            pair_s.at[c],
            pair_r.at[c],
            partner,
        )

    def chain_copy(c):
        return remote(
            chain_out.at[c], chain_in.at[c], chain_s.at[c], chain_r.at[c],
            {"section": section - 2},
        )

    def swap_copy(c):
        return remote(swap_out.at[c], swap_in.at[c], swap_s.at[c], swap_r.at[c], partner)

    def rows_copy(c):
        return remote(
            rows_out.at[c], rows_all.at[core, c], rows_s.at[c], rows_r.at[c], other_core
        )

    def part_copy(m):
        return remote(part_out.at[m], part_in.at[m], part_s.at[m], part_r.at[m], other_shard)

    ex_copy = remote(ex_out, ex_all.at[core], one_s.at[0], one_r.at[0], other_core)
    hid_copy = remote(hid_own, hid_in, one_s.at[1], one_r.at[1], other_shard)

    for c in range(min(IN_FLIGHT, chunks)):
        stage_load(c).wait()
        pair_copy(c).start()
    hidden_load.start()
    basis_load.start()
    top_load.start()
    model_load.start()

    def slot_tables():
        lane_token = lax.broadcasted_iota(jnp.int32, (tokens, tokens), 1)
        row_token = lax.broadcasted_iota(jnp.int32, (tokens, tokens), 0)
        slot_row = lax.broadcasted_iota(jnp.int32, (cap, tokens), 0).astype(jnp.float32)
        select_v[...] = jnp.zeros_like(select_v)
        for load in small_loads:
            load.wait()
        for m in range(batches):
            named = routes_v[0, m]
            weight = probs_v[0, m]
            example_row = examples_v[m].astype(jnp.float32)
            for place in range(2):
                expert = core if place == 0 else 1 - core
                hit = named == expert
                count_row = jnp.sum(jnp.where(hit, 1.0, 0.0), axis=0, keepdims=True)
                prob_row = jnp.sum(jnp.where(hit, weight, 0.0), axis=0, keepdims=True)
                count = jnp.sum(
                    jnp.where(row_token == lane_token, count_row, 0.0), axis=1, keepdims=True
                )
                rank_row = jnp.sum(
                    jnp.where(row_token < lane_token, count, 0.0), axis=0, keepdims=True
                )
                match = jnp.where(slot_row == rank_row, 1.0, 0.0) * count_row
                slot_prob = jnp.sum(match * prob_row, axis=1, keepdims=True)
                slot_example = jnp.sum(match * (example_row + 1.0), axis=1, keepdims=True) - 1.0
                first = place * rows + m * cap
                for at in (m * tokens, flat + m * tokens):
                    select_v[first : first + cap, at : at + tokens] = match.astype(jnp.bfloat16)
                prob_v[first : first + cap, :] = jnp.broadcast_to(slot_prob, (cap, prob_v.shape[1]))
                wide = jnp.broadcast_to(slot_example.astype(jnp.int32), (cap, ex_out.shape[2]))
                if place == 0:
                    ex_all[core, m] = wide
                else:
                    ex_out[m] = wide
        ex_copy.start()

    @pl.when(high < last)
    def _():
        slot_tables()

    @pl.when(high == last)
    def _():
        chain_in[...] = jnp.zeros_like(chain_in)

    own_load.wait()

    def feed(c):
        @pl.when(c + IN_FLIGHT < chunks)
        def _():
            pair_copy(c).wait_send()
            stage_load(c + IN_FLIGHT).wait()
            pair_copy(c + IN_FLIGHT).start()

    def carry(c):
        pair_copy(c).wait_recv()

        @pl.when(high < last)
        def _():
            chain_copy(c).wait_recv()

        own = own_v[:, :, pl.ds(pl.multiple_of(c * chunk, 128), chunk)].astype(jnp.float32)
        before = chain_in[c].astype(jnp.float32)

        @pl.when(high > 0)
        def _():
            total = before + own + pair_in[c].astype(jnp.float32)
            chain_out[c] = total.astype(jnp.bfloat16)
            chain_copy(c).start()

        swap_out[c] = (before + jnp.where(low == 1, own, 0.0)).astype(jnp.bfloat16)

    def rotate_hidden():
        hidden_load.wait()
        basis_load.wait()
        hid_own[...] = jnp.zeros_like(hid_own)

        def piece(p, _):
            acts = hidden_v[:, :, pl.ds(pl.multiple_of(p * piece_depth, 128), piece_depth)]
            hid_own[...] += jnp.dot(
                acts.reshape(batches * acts.shape[1], piece_depth),
                bh_v[pl.ds(pl.multiple_of(p * piece_depth, 128), piece_depth), :],
                preferred_element_type=jnp.float32,
            )
            return 0

        lax.fori_loop(0, pieces, piece, 0)
        hid_copy.start()

    def dispatch(c):
        swap_copy(c).wait_recv()
        select = select_v[...]
        slot_prob = jnp.concatenate([prob_v[...]] * (chunk // prob_v.shape[1]), axis=1)

        def picked(cotangent):
            wide = cotangent.reshape(flat, chunk)
            coarse = wide.astype(jnp.bfloat16)
            fine = (wide - coarse.astype(jnp.float32)).astype(jnp.bfloat16)
            found = jnp.dot(
                select,
                jnp.concatenate([coarse, fine], axis=0),
                preferred_element_type=jnp.float32,
            )
            return (found * slot_prob).astype(jnp.bfloat16)

        def wide_top(half_index):
            return top_v[:, :, columns(half_index, c)].astype(jnp.float32)

        pair_term = jnp.where(low == 0, pair_in[c].astype(jnp.float32), 0.0)
        mine = picked(wide_top(low) + chain_in[c].astype(jnp.float32) + pair_term)
        rest = picked(wide_top(1 - low) + swap_in[c].astype(jnp.float32))
        rows_out[c, low] = mine[rows:]
        rows_out[c, 1 - low] = rest[rows:]
        rows_copy(c).start()
        rows_all[core, c, low] = mine[:rows]
        rows_all[core, c, 1 - low] = rest[:rows]

    batch = 2 if chunks % 2 == 0 else 1

    def rotate_model(index):
        each = [(index * batch + part, h) for part in range(batch) for h in range(2)]
        for part in range(batch):
            rows_copy(index * batch + part).wait_recv()
        total = jnp.dot(
            jnp.concatenate(
                [
                    jnp.concatenate([rows_all[0, c, h], rows_all[1, c, h]], axis=0)
                    for c, h in each
                ],
                axis=1,
            ),
            jnp.concatenate(
                [
                    bm_v[pl.ds(pl.multiple_of(h * half + c * chunk, 128), chunk), :]
                    for c, h in each
                ],
                axis=0,
            ),
            preferred_element_type=jnp.float32,
        )

        @pl.when(index == 0)
        def _():
            model_sum[...] = total

        @pl.when(index > 0)
        def _():
            model_sum[...] += total

    def block_columns(index):
        return pl.ds(pl.multiple_of(index * cols, 128), cols)

    turns = cap // 2 + 1

    def padding(like):
        return [jnp.zeros((hid_t.shape[2] - group * 2 * turns * cap, like.shape[1]), jnp.float32)]

    def prepare_hidden():
        ex_copy.wait_recv()
        hid_copy.wait_recv()
        hid = (hid_own[...] + hid_in[...]).astype(jnp.bfloat16).astype(jnp.float32)
        for part in range(batches // group):
            blocks = []
            for m in range(part * group, (part + 1) * group):
                for owner in range(2):
                    first = m * 2 * cap + owner * cap
                    block = hid[first : first + cap]
                    ids = ex_all[owner, m].astype(jnp.float32)
                    for turn in range(turns):
                        share = 1.0 if turn in (0, cap // 2) else 2.0
                        if turn:
                            other = pltpu.roll(block, turn, 0)
                            other_ids = pltpu.roll(ids, turn, 0)
                        else:
                            other, other_ids = block, ids
                        same = jnp.where(ids == other_ids, share, 0.0)
                        blocks.append(block * other * same[:, :1])
            pairs = jnp.concatenate(blocks + padding(hid), axis=0)
            hid_t[part] = pairs.T.astype(jnp.bfloat16)

    def squares(part):
        blocks = []
        for m in range(part * group, (part + 1) * group):
            part_copy(m).wait_recv()
            for owner in range(2):
                first = owner * rows + m * cap
                block = model_sum[first : first + cap, block_columns(shard)]
                block = block + part_in[m, owner].astype(jnp.float32)
                block = block.astype(jnp.bfloat16).astype(jnp.float32)
                for turn in range(turns):
                    other = pltpu.roll(block, turn, 0) if turn else block
                    blocks.append(block * other)
        pairs = jnp.concatenate(blocks + padding(blocks[0]), axis=0).astype(jnp.bfloat16)
        return jnp.dot(hid_t[part], pairs, preferred_element_type=jnp.float32)

    early = high < last - 1
    held = jnp.minimum(chunks - 1, HOP_LAG * high)
    lag = jnp.where(high > 0, jnp.maximum(chunks, held + SWAP_LAG), held + SWAP_LAG)
    model_lag = lag + ROWS_LAG - 1

    @pl.when(early)
    def _():
        rotate_hidden()

    @pl.when(high < last)
    def _():
        lax.fori_loop(0, chunks, lambda c, _: (feed(c), 0)[1], 0)

    @pl.when(high == 0)
    def _():
        @pl.when(jnp.logical_not(early))
        def _():
            rotate_hidden()

        prepare_hidden()

    def step(k, _):
        @pl.when(k < chunks)
        def _():
            carry(k)

            @pl.when(high == last)
            def _():
                feed(k)

        @pl.when(jnp.logical_and(k >= held, k < chunks + held))
        def _():
            swap_copy(k - held).start()

        @pl.when(jnp.logical_and(k == chunks - 1, high == last))
        def _():
            slot_tables()

        @pl.when(jnp.logical_and(k == chunks - 1, jnp.logical_not(early)))
        def _():
            @pl.when(high > 0)
            def _():
                rotate_hidden()

        @pl.when(jnp.logical_and(k == chunks + 1, high > 0))
        def _():
            prepare_hidden()

        @pl.when(k == lag)
        def _():
            top_load.wait()
            model_load.wait()

        @pl.when(jnp.logical_and(k >= lag, k < chunks + lag))
        def _():
            dispatch(k - lag)

        ready = k - model_lag

        @pl.when(jnp.logical_and(ready >= 0, lax.rem(ready + batch, batch) == batch - 1))
        def _():
            rotate_model(ready // batch)

        return 0

    lax.fori_loop(0, chunks + model_lag, step, 0)

    for m in range(batches):
        for owner in range(2):
            first = owner * rows + m * cap
            part_out[m, owner] = model_sum[
                first : first + cap, block_columns(1 - shard)
            ].astype(jnp.bfloat16)
        part_copy(m).start()
    out[0, 0] = squares(0)
    for part in range(1, batches // group):
        out[0, 0] += squares(part)

    for c in range(chunks):
        swap_copy(c).wait_send()
        rows_copy(c).wait_send()
    for c in range(max(chunks - IN_FLIGHT, 0), chunks):
        pair_copy(c).wait_send()
    for m in range(batches):
        part_copy(m).wait_send()
    ex_copy.wait_send()
    hid_copy.wait_send()

    @pl.when(high > 0)
    def _():
        for c in range(chunks):
            chain_copy(c).wait_send()


def on_device(
    routes,
    route_probs,
    example_ids,
    top_cotangent,
    branch_cotangent,
    hidden_acts,
    basis_hidden,
    basis_model,
):
    sections = lax.axis_size("section")
    shards = lax.axis_size("shard")
    batches, tokens, width = top_cotangent.shape
    slots, depth = hidden_acts.shape[3:]
    cap = slots // lax.axis_size("expert")
    rank_hidden = basis_hidden.shape[3]
    cols = basis_model.shape[3] // shards
    half = width // 2
    chunk = CHUNK if half % CHUNK == 0 else 128
    chunks = half // chunk
    group = 2 if batches % 2 == 0 else 1
    pairs = -(-group * 2 * (cap // 2 + 1) * cap // 128) * 128
    bf16, f32 = jnp.bfloat16, jnp.float32
    vmem = pl.BlockSpec(memory_space=pltpu.VMEM)
    hbm = pl.BlockSpec(memory_space=pl.ANY)
    dma = pltpu.SemaphoreType.DMA
    moving = pltpu.VMEM((chunks, batches, tokens, chunk), bf16)
    routes = jnp.swapaxes(routes, 2, 3)
    route_probs = jnp.swapaxes(route_probs, 2, 3)
    flops = 2 * batches * slots * (depth * rank_hidden + width * cols * shards)
    square_sum = pl.pallas_call(
        functools.partial(kernel, sections),
        out_shape=jax.ShapeDtypeStruct((1, 1, rank_hidden, cols), f32),
        in_specs=[hbm] * 8,
        out_specs=vmem,
        scratch_shapes=[
            pltpu.VMEM(routes.shape, jnp.int32),
            pltpu.VMEM(route_probs.shape, f32),
            pltpu.VMEM(example_ids.shape, jnp.int32),
            pltpu.VMEM((batches, tokens, width), bf16),
            pltpu.VMEM((batches, tokens, half), bf16),
            moving,
            pltpu.VMEM((batches, slots, depth), bf16),
            pltpu.VMEM((depth, rank_hidden), bf16),
            pltpu.VMEM((width, cols * shards), bf16),
            moving,
            moving,
            moving,
            moving,
            moving,
            pltpu.VMEM((2 * batches * cap, 2 * batches * tokens), bf16),
            pltpu.VMEM((2 * batches * cap, 128), f32),
            pltpu.VMEM((batches, cap, 128), jnp.int32),
            pltpu.VMEM((2, batches, cap, 128), jnp.int32),
            pltpu.VMEM((chunks, 2, batches * cap, chunk), bf16),
            pltpu.VMEM((2, chunks, 2, batches * cap, chunk), bf16),
            pltpu.VMEM((batches * slots, cols * shards), f32),
            pltpu.VMEM((batches, 2, cap, cols), bf16),
            pltpu.VMEM((batches, 2, cap, cols), bf16),
            pltpu.VMEM((batches * slots, rank_hidden), f32),
            pltpu.VMEM((batches * slots, rank_hidden), f32),
            pltpu.VMEM((batches // group, rank_hidden, pairs), bf16),
            dma((8,)),
        ]
        + [dma((chunks,))] * 9
        + [dma((batches,))] * 2
        + [dma((2,))] * 2,
        compiler_params=pltpu.CompilerParams(
            collective_id=0, has_side_effects=True, vmem_limit_bytes=60 * 1024 * 1024
        ),
        cost_estimate=pl.CostEstimate(
            flops=flops, bytes_accessed=16 * 1024 * 1024, transcendentals=0
        ),
    )(
        routes,
        route_probs,
        example_ids,
        top_cotangent,
        branch_cotangent,
        hidden_acts,
        basis_hidden,
        basis_model,
    )
    return square_sum / (batches * lax.axis_size("expert") * SEQS)


def solution(mesh):
    return jax.shard_map(
        on_device,
        mesh=mesh,
        in_specs=(
            P("section", None, "expert", None),
            P("section", None, "expert", None),
            P(None, "expert", None),
            P(None, "expert", "shard"),
            P("section", None, "expert", "shard"),
            P("section", "expert", None, None, "shard"),
            P("section", "expert", "shard", None),
            P("section", "expert", "shard", None),
        ),
        out_specs=P("section", "expert", None, "shard"),
        check_vma=False,
    )
```
